32 devices in a mesh: seq: 8 (over y, x, core), tok: 4 (over z).
Axes of the slice: x: 2, y: 2, z: 4, core: 2. Of those that a mesh axis runs over, the one named last changes fastest.
Arguments:
- entering: bfloat16 [8, 512, 3, 512], P('seq', 'tok'), may hold values from -0.9059806 to 0.9059806, as said below
- fresh: bfloat16 [512, 3, 512], P('tok'), may hold values from -0.9059806 to 0.9059806, as said below
- qkv_first: bfloat16 [8, 2048, 3, 512], P('seq', 'tok'), may hold values from -6 to 6
- qkv_second: bfloat16 [8, 2048, 3, 512], P('seq', 'tok'), may hold values from -6 to 6
- rates_first: float32 [8, 2048], P('seq', 'tok'), may hold values from 0.00011048543 to 0.0011048544
- rates_second: float32 [8, 2048], P('seq', 'tok'), may hold values from 0.00011048543 to 0.0011048544
Outputs:
- out_first: bfloat16 [8, 2048, 512], P('seq', 'tok')
- out_second: bfloat16 [8, 2048, 512], P('seq', 'tok')
- leaving: bfloat16 [8, 512, 3, 512], P('seq', 'tok')
The draws below stay inside these ranges and needn't reach their ends.
Inputs may be any that keep to these rules, and one draw needn't show every extreme that they name: `entering`: fast weights of a scale near 512 ** -0.5. `fresh`: fast weights of a scale near 512 ** -0.5.
All inputs are finite; a program needn't handle non-finite values.
Results may differ from the reference program's by a relative error of at most 0.02.
Values may be sent and summed in bfloat16 or wider, within the bound.
A program may use at most 64 MiB of HBM per device.

```python
import math
import jax
import jax.numpy as jnp
from jax import lax

D = 512
FF = 512
TOK_DEV = 512
SPAN = 2048
N_SEQ = 8
N_TOK = 4


def weight_block(key, leading):
    key_noise, key_rows, key_cols = jax.random.split(key, 3)
    shape = leading + (FF, 3, D)
    normal_part = jnp.clip(jax.random.normal(key_noise, shape, jnp.float32), -4.0, 4.0)
    low = math.log(0.32)
    high = math.log(3.2)
    row_scale = jnp.exp(jax.random.uniform(key_rows, leading + (FF, 3, 1), jnp.float32, low, high))
    col_scale = jnp.exp(jax.random.uniform(key_cols, leading + (1, 3, D), jnp.float32, low, high))
    return (normal_part * row_scale * col_scale * (0.5 / math.sqrt(D))).astype(jnp.bfloat16)


def draw_entering(key, part):
    return weight_block(jax.random.fold_in(key, 11), (N_SEQ,))


def draw_fresh(key, part):
    return weight_block(jax.random.fold_in(key, 12), ())


def steps_of(key, extent, cuts, smallest, largest):
    loudness = 1.0
    for position, parts in cuts:
        steps = jax.random.uniform(jax.random.fold_in(jax.random.fold_in(key, 6), position), (parts,), jnp.float32, smallest / len(cuts), largest / len(cuts))
        loudness = loudness * jnp.repeat(jnp.exp(steps), extent[position] // parts).reshape((-1,) + (1,) * (len(extent) - 1 - position))
    return loudness


def centred(stream_key, extent, scale, reach, shards=(), held_as=jnp.bfloat16):
    result = jax.random.normal(stream_key, extent, jnp.float32) * scale
    if len(shards) > 0:
        result = steps_of(stream_key, extent, shards, -0.22, 0.18) * result
    return jnp.clip(result, min=-reach, max=reach).astype(held_as)


def setup_inputs(seed: int = 0) -> dict:
    splits = jax.random.split(jax.random.key(seed), 7)
    entering = draw_entering(jax.random.fold_in(splits[6], 71), 0)
    fresh = draw_fresh(jax.random.fold_in(splits[6], 71), 0)
    qkv_first = centred(splits[2], (N_SEQ, SPAN, 3, D), 1.0, 6.0, ((0, 8), (1, 4)))
    qkv_second = centred(splits[3], (N_SEQ, SPAN, 3, D), 1.0, 6.0, ((0, 8), (1, 4)))
    rates_first = jnp.clip(jnp.exp(math.log(0.0011048544) - 2.3025852 * jax.random.uniform(splits[4], (N_SEQ, SPAN), jnp.float32) ** steps_of(splits[4], (N_SEQ, SPAN), ((0, 8), (1, 4)), -0.2, 0.2)), 0.00011048543, 0.0011048544)
    rates_second = jnp.clip(jnp.exp(math.log(0.0011048544) - 2.3025852 * jax.random.uniform(splits[5], (N_SEQ, SPAN), jnp.float32) ** steps_of(splits[5], (N_SEQ, SPAN), ((0, 8), (1, 4)), -0.2, 0.2)), 0.00011048543, 0.0011048544)
    return {"entering": entering, "fresh": fresh, "qkv_first": qkv_first, "qkv_second": qkv_second, "rates_first": rates_first, "rates_second": rates_second}


def forward_rows(weights, inputs):
    pre_gate = jnp.dot(inputs, weights[:, 0, :].T, preferred_element_type=jnp.float32)
    pre_up = jnp.dot(inputs, weights[:, 1, :].T, preferred_element_type=jnp.float32)
    return (pre_gate, pre_up)

def renormed(weights, gradient):
    old_values = weights.astype(jnp.float32)
    stepped = old_values - gradient
    old_norm = jnp.sqrt(lax.optimization_barrier(jnp.sum(old_values * old_values, axis=-1, keepdims=True)))
    new_norm = jnp.sqrt(lax.optimization_barrier(jnp.sum(stepped * stepped, axis=-1, keepdims=True)) + 1e-06)
    return (stepped * (old_norm / new_norm)).astype(jnp.bfloat16)

def fast_tick(weights, tick_data, token_rates):
    queries = tick_data[:, 0, :]
    key_rows = tick_data[:, 1, :]
    value_rows = tick_data[:, 2, :]
    gate_q, up_q = forward_rows(weights, queries)
    hidden_q = (jax.nn.silu(gate_q) * up_q).astype(jnp.bfloat16)
    output = jnp.dot(hidden_q, weights[:, 2, :], preferred_element_type=jnp.float32).astype(jnp.bfloat16)
    gate_k, up_k = forward_rows(weights, key_rows)
    hidden_k = (jax.nn.silu(gate_k) * up_k).astype(jnp.bfloat16)
    scaled = (-token_rates[:, None] * value_rows.astype(jnp.float32)).astype(jnp.bfloat16)
    d_hidden = jnp.dot(scaled, weights[:, 2, :].T, preferred_element_type=jnp.float32)
    sigmoid_gate = jax.nn.sigmoid(gate_k)
    d_gate = (d_hidden * up_k * sigmoid_gate * (1.0 + gate_k * (1.0 - sigmoid_gate))).astype(jnp.bfloat16)
    d_up = (d_hidden * jax.nn.silu(gate_k)).astype(jnp.bfloat16)
    width = key_rows.shape[1]
    hidden_units = weights.shape[0]

    def blocks(array):
        return array.reshape(N_TOK, TOK_DEV, array.shape[1])

    def add_partial(running, pieces):
        gate_piece, up_piece, hidden_piece, key_piece, scaled_piece = pieces
        partial_value = jnp.stack([jnp.dot(gate_piece.T, key_piece, preferred_element_type=jnp.float32), jnp.dot(up_piece.T, key_piece, preferred_element_type=jnp.float32), jnp.dot(hidden_piece.T, scaled_piece, preferred_element_type=jnp.float32)], axis=1)
        rounded = lax.optimization_barrier(partial_value.astype(jnp.bfloat16))
        return (running + rounded.astype(jnp.float32), None)
    start = jnp.zeros((hidden_units, 3, width), jnp.float32)
    gradient, _ = lax.scan(add_partial, start, (blocks(d_gate), blocks(d_up), blocks(hidden_k), blocks(key_rows), blocks(scaled)))
    return (output, renormed(weights, gradient))

def group_tick(inputs):
    return fast_tick(inputs[0], inputs[1], inputs[2])

def reference(entering, fresh, qkv_first, qkv_second, rates_first, rates_second):
    out_first, updated = lax.map(group_tick, (entering, qkv_first, rates_first))
    passed = jnp.concatenate([fresh[None], updated[:-1]], axis=0)
    out_second, leaving = lax.map(group_tick, (passed, qkv_second, rates_second))
    return (out_first, out_second, leaving)
```

```python
import functools
import jax
import jax.numpy as jnp
from jax import lax
from jax.experimental import pallas as pl
from jax.experimental.pallas import tpu as pltpu
from jax.sharding import PartitionSpec as P

MESH = pl.DeviceIdType.MESH
NT = (((1,), (1,)), ((), ()))
NN = (((1,), (0,)), ((), ()))


def dot(a, b, dims):
    return lax.dot_general(a, b, dims, preferred_element_type=jnp.float32)


def kernel(
    n, nseq, m, period,
    ent, fresh, x_first, x_second, rates_first, rates_second,
    out_first, out_second, leaving,
    wbuf, rl, rr, part, xbuf, acc, ubuf,
    x_sem, w_recv, w_send_r, w_send_l, rl_recv, rl_send, rr_recv, rr_send, n_send, n_recv,
):
    rounds = 2 * period
    s = lax.axis_index("seq")
    p = lax.axis_index("tok")
    when = pl.when
    has_left, has_right = p > 0, p < n - 1
    has_prev, has_next = s > 0, s < nseq - 1
    left, right = (s, jnp.maximum(p - 1, 0)), (s, jnp.minimum(p + 1, n - 1))
    prev, following = (jnp.maximum(s - 1, 0), p), (jnp.minimum(s + 1, nseq - 1), p)
    block, width = wbuf.shape[3:]
    units = n * block

    def rows(r):
        return pl.ds(pl.multiple_of(r * block, block), block)

    def load_x(t):
        src = x_first if t == 0 else x_second
        return pltpu.make_async_copy(src, xbuf.at[t], x_sem.at[t])

    load_x(0).start()
    load_x(1).start()

    barrier = pltpu.get_barrier_semaphore()
    for there, device in ((has_left, left), (has_right, right), (has_prev, prev), (has_next, following)):
        @when(there)
        def _():
            pl.semaphore_signal(barrier, inc=1, device_id=device, device_id_type=MESH)
    for r in range(m):
        wbuf[r, p] = ent[:, r * block:(r + 1) * block]
    peers = sum(jnp.where(there, 1, 0) for there in (has_left, has_right, has_prev, has_next))
    pl.semaphore_wait(barrier, peers)

    def valid(i):
        return jnp.logical_and(jnp.logical_and(i >= 0, i < rounds), lax.rem(i + period, period) < m)

    def w_right(g, j):
        return pltpu.make_async_remote_copy(
            wbuf.at[g, j], wbuf.at[g, j], w_send_r.at[g, j], w_recv.at[g, j], device_id=right, device_id_type=MESH)

    def w_left(g, j):
        return pltpu.make_async_remote_copy(
            wbuf.at[g, j], wbuf.at[g, j], w_send_l.at[g, j], w_recv.at[g, j], device_id=left, device_id_type=MESH)

    def sum_right(g, j):
        return pltpu.make_async_remote_copy(
            rl.at[g, j], rl.at[g, j], rl_send.at[g, j], rl_recv.at[g, j], device_id=right, device_id_type=MESH)

    def sum_left(g, j):
        return pltpu.make_async_remote_copy(
            rr.at[g, j], rr.at[g, j], rr_send.at[g, j], rr_recv.at[g, j], device_id=left, device_id_type=MESH)

    def hand_on(r):
        return pltpu.make_async_remote_copy(
            ubuf.at[r], wbuf.at[period + r, p], n_send.at[r], n_recv.at[r], device_id=following, device_id_type=MESH)

    def w_start(g):
        @when(g >= period)
        def _():
            @when(has_prev)
            def _():
                hand_on(g - period).wait_recv()

            @when(jnp.logical_not(has_prev))
            def _():
                wbuf[g, p] = fresh[:, rows(g - period)]

        @when(has_right)
        def _():
            w_right(g, p).start()

        @when(has_left)
        def _():
            w_left(g, p).start()

    def w_hop(g, h):
        @when(p >= h)
        def _():
            w_right(g, p - h).wait_recv()

            @when(has_right)
            def _():
                w_right(g, p - h).start()

        @when(p + h < n)
        def _():
            w_left(g, p + h).wait_recv()

            @when(has_left)
            def _():
                w_left(g, p + h).start()

    def sum_hop(g, h):
        own = part.at[lax.rem(g, 2)]

        @when(p == h)
        def _():
            for j in range(n - 1, h, -1):
                value = own[j]
                if h > 0:
                    sum_right(g, j).wait_recv()
                    value = value + rl[g, j].astype(jnp.float32)
                rl[g, j] = value.astype(jnp.bfloat16)
                sum_right(g, j).start()

        @when(p == n - 1 - h)
        def _():
            for j in range(n - 1 - h):
                value = own[j]
                if h > 0:
                    sum_left(g, j).wait_recv()
                    value = value + rr[g, j].astype(jnp.float32)
                rr[g, j] = value.astype(jnp.bfloat16)
                sum_left(g, j).start()

    def update(g):
        for there, edge, buf, arrival in (
            (has_left, p == 0, rl, sum_right),
            (has_right, p == n - 1, rr, sum_left),
        ):
            @when(there)
            def _():
                arrival(g, p).wait_recv()

            @when(edge)
            def _():
                buf[g, p] = jnp.zeros(buf.shape[2:], buf.dtype)
        gradient = part[lax.rem(g, 2), p] + rl[g, p].astype(jnp.float32) + rr[g, p].astype(jnp.float32)
        old = wbuf[g, p].astype(jnp.float32)
        stepped = old - gradient
        old_norm = jnp.sqrt(jnp.sum(old * old, axis=-1, keepdims=True))
        new_norm = jnp.sqrt(jnp.sum(stepped * stepped, axis=-1, keepdims=True) + 1e-06)
        new = (stepped * (old_norm / new_norm)).astype(jnp.bfloat16)

        @when(g < period)
        def _():
            ubuf[g] = new

            @when(has_next)
            def _():
                hand_on(g).start()

        @when(g >= period)
        def _():
            leaving[:, rows(g - period)] = new

    def key_part(i):
        t = lax.div(i, period)
        keys, scaled = xbuf[t, 1], xbuf[t, 2]
        w_gu = wbuf[i, :, 0:2].reshape(2 * units, width)
        w_d = wbuf[i, :, 2].reshape(units, width)
        pre = dot(w_gu, keys, NT).reshape(n, 2, units // n, -1)
        gate, up = pre[:, 0], pre[:, 1]
        d_hidden = dot(w_d, scaled, NT).reshape(gate.shape)
        sig = 1.0 / (1.0 + jnp.exp(-gate))
        act = gate * sig
        hidden = (act * up).astype(jnp.bfloat16).reshape(units, -1)
        d_gate = (d_hidden * up * (sig * (1.0 + gate * (1.0 - sig)))).astype(jnp.bfloat16)
        d_up = (d_hidden * act).astype(jnp.bfloat16)
        d_gu = jnp.stack([d_gate, d_up], axis=1).reshape(2 * units, -1)
        slot = lax.rem(i, 2)
        part[slot, :, 0:2] = dot(d_gu, keys, NN).reshape(n, 2, units // n, width)
        part[slot, :, 2] = dot(hidden, scaled, NN).reshape(n, units // n, width)

    def query_part(i):
        t = lax.div(i, period)
        r = lax.rem(i, period)
        w_gu = jnp.concatenate(
            [wbuf[i, :, 0].reshape(units, width), wbuf[i, :, 1].reshape(units, width)], axis=0)
        pre = dot(xbuf[t, 0], w_gu, NT)
        gate, up = pre[:, :units], pre[:, units:]
        hidden = (gate / (1.0 + jnp.exp(-gate)) * up).astype(jnp.bfloat16)
        out = dot(hidden, wbuf[i, :, 2].reshape(units, width), NN)

        @when(r == 0)
        def _():
            acc[...] = out

        @when(r > 0)
        def _():
            acc[...] += out

        @when(r == m - 1)
        def _():
            @when(t == 0)
            def _():
                out_first[...] = acc[...].astype(jnp.bfloat16)

            @when(t == 1)
            def _():
                out_second[...] = acc[...].astype(jnp.bfloat16)

    cut = (n + 1) // 3
    w_groups = (range(1, 1 + cut), range(1 + cut, 1 + 2 * cut), range(1 + 2 * cut, n))
    half = 1 + n // 2 - 1 if n > 2 else 1
    s_groups = (range(1, half), range(half, n - 1))

    w_start(0)
    w_start(1)

    def slot(step, carry):
        i = step - 1

        @when(valid(i))
        def _():
            for h in w_groups[2]:
                w_hop(i, h)

        def middle(which):
            @when(valid(i + 1))
            def _():
                for h in w_groups[which]:
                    w_hop(i + 1, h)

            @when(valid(i - 1))
            def _():
                for h in s_groups[which]:
                    sum_hop(i - 1, h)

        middle(0)

        @when(valid(i))
        def _():
            for t in range(2):
                @when(i == t * period)
                def _():
                    load_x(t).wait()
                    rates = (rates_first, rates_second)[t][...]
                    column = jnp.broadcast_to(rates, (8, rates.shape[1])).T[:, 0:1]
                    xbuf[t, 2] = (-column * xbuf[t, 2].astype(jnp.float32)).astype(jnp.bfloat16)
            key_part(i)
            sum_hop(i, 0)

        @when(jnp.logical_and(i >= 0, valid(i + 2)))
        def _():
            w_start(i + 2)

        middle(1)

        @when(valid(i))
        def _():
            query_part(i)

        @when(valid(i - 1))
        def _():
            update(i - 1)

        return carry

    lax.fori_loop(0, rounds + 2, slot, 0)

    def drain(g, carry):
        @when(valid(g))
        def _():
            for j in range(n):
                @when(jnp.logical_and(j <= p, has_right))
                def _():
                    w_right(g, j).wait_send()

                @when(jnp.logical_and(j >= p, has_left))
                def _():
                    w_left(g, j).wait_send()

                @when(j > p)
                def _():
                    sum_right(g, j).wait_send()

                @when(j < p)
                def _():
                    sum_left(g, j).wait_send()

            @when(jnp.logical_and(g < period, has_next))
            def _():
                hand_on(g).wait_send()

        return carry

    lax.fori_loop(0, rounds, drain, 0)


def on_device(n, nseq, entering, fresh, qkv_first, qkv_second, rates_first, rates_second):
    rows, _, width = fresh.shape
    tokens = qkv_first.shape[1]
    m = min(4, rows // 16)
    period = max(m, 4)
    block = rows // m

    bf16, f32 = jnp.bfloat16, jnp.float32
    vmem = pl.BlockSpec(memory_space=pltpu.VMEM)
    anywhere = pl.BlockSpec(memory_space=pl.ANY)
    rounds = 2 * period
    chunk = (3, block, width)
    dma = pltpu.SemaphoreType.DMA
    out_first, out_second, leaving = pl.pallas_call(
        functools.partial(kernel, n, nseq, m, period),
        out_shape=(
            jax.ShapeDtypeStruct((tokens, width), bf16),
            jax.ShapeDtypeStruct((tokens, width), bf16),
            jax.ShapeDtypeStruct((3, rows, width), bf16),
        ),
        in_specs=[vmem, vmem, anywhere, anywhere, vmem, vmem],
        out_specs=(vmem, vmem, vmem),
        scratch_shapes=[
            pltpu.VMEM((rounds, n) + chunk, bf16),
            pltpu.VMEM((rounds, n) + chunk, bf16),
            pltpu.VMEM((rounds, n) + chunk, bf16),
            pltpu.VMEM((2, n) + chunk, f32),
            pltpu.VMEM((2, 3, tokens, width), bf16),
            pltpu.VMEM((tokens, width), f32),
            pltpu.VMEM((m,) + chunk, bf16),
            dma((2,)),
        ] + [dma((rounds, n))] * 7 + [dma((m,)), dma((m,))],
        compiler_params=pltpu.CompilerParams(
            collective_id=0, has_side_effects=True, vmem_limit_bytes=48 * 1024 * 1024),
    )(
        entering[0].transpose(1, 0, 2), fresh.transpose(1, 0, 2),
        qkv_first[0].transpose(1, 0, 2), qkv_second[0].transpose(1, 0, 2), rates_first, rates_second,
    )
    leaving = leaving.transpose(1, 0, 2)
    return (out_first[None], out_second[None], leaving[None])


def solution(mesh):
    placed = (
        P("seq", "tok", None, None),
        P("tok", None, None),
        P("seq", "tok", None, None),
        P("seq", "tok", None, None),
        P("seq", "tok"),
        P("seq", "tok"),
    )
    return jax.shard_map(
        functools.partial(on_device, mesh.shape["tok"], mesh.shape["seq"]),
        mesh=mesh,
        in_specs=placed,
        out_specs=(P("seq", "tok", None), P("seq", "tok", None), P("seq", "tok", None, None)),
        check_vma=False,
    )
```

```python
import functools
import jax
import jax.numpy as jnp
from jax import lax
from jax.experimental import pallas as pl
from jax.experimental.pallas import tpu as pltpu
from jax.sharding import PartitionSpec as P

MESH = pl.DeviceIdType.MESH
NT = (((1,), (1,)), ((), ()))
NN = (((1,), (0,)), ((), ()))


def dot(a, b, dims):
    return lax.dot_general(a, b, dims, preferred_element_type=jnp.float32)


def kernel(
    n, nseq, m, period,
    ent, fresh, x_first, x_second, rates_first, rates_second,
    out_first, out_second, leaving,
    wbuf, rl, rr, part, xbuf, acc, ubuf,
    fresh_buf, x_sem, own_sem, fresh_sem, w_recv, w_send_r, w_send_l, rl_recv, rl_send, rr_recv, rr_send, n_send, n_recv,
):
    rounds = 2 * period
    s = lax.axis_index("seq")
    p = lax.axis_index("tok")
    when = pl.when
    has_left, has_right = p > 0, p < n - 1
    has_prev, has_next = s > 0, s < nseq - 1
    left, right = (s, jnp.maximum(p - 1, 0)), (s, jnp.minimum(p + 1, n - 1))
    prev, following = (jnp.maximum(s - 1, 0), p), (jnp.minimum(s + 1, nseq - 1), p)
    block, width = wbuf.shape[3:]
    units = n * block
    group = 2 if m % 2 == 0 else 1

    def rows(r):
        return pl.ds(pl.multiple_of(r * block, block), block)

    def load_x(t):
        src = x_first if t == 0 else x_second
        return pltpu.make_async_copy(src, xbuf.at[t], x_sem.at[t])

    def load_own(r):
        return pltpu.make_async_copy(ent.at[:, r * block:(r + 1) * block], wbuf.at[r, p], own_sem.at[r])

    load_fresh = pltpu.make_async_copy(fresh, fresh_buf, fresh_sem)

    for r in range(m):
        load_own(r).start()
    load_x(0).start()
    load_x(1).start()
    load_fresh.start()

    barrier = pltpu.get_barrier_semaphore()
    for there, device in ((has_left, left), (has_right, right), (has_prev, prev), (has_next, following)):
        @when(there)
        def _():
            pl.semaphore_signal(barrier, inc=1, device_id=device, device_id_type=MESH)
    for r in range(m):
        load_own(r).wait()
    load_fresh.wait()
    peers = sum(jnp.where(there, 1, 0) for there in (has_left, has_right, has_prev, has_next))
    pl.semaphore_wait(barrier, peers)

    def valid(i):
        return jnp.logical_and(jnp.logical_and(i >= 0, i < rounds), lax.rem(i + period, period) < m)

    def index(i):
        return lax.div(i, period) * m + lax.rem(i, period)

    def w_right(g, j):
        return pltpu.make_async_remote_copy(
            wbuf.at[g, j], wbuf.at[g, j], w_send_r.at[g, j], w_recv.at[g, j], device_id=right, device_id_type=MESH)

    def w_left(g, j):
        return pltpu.make_async_remote_copy(
            wbuf.at[g, j], wbuf.at[g, j], w_send_l.at[g, j], w_recv.at[g, j], device_id=left, device_id_type=MESH)

    def sum_right(g, j):
        return pltpu.make_async_remote_copy(
            rl.at[g, j], rl.at[g, j], rl_send.at[g, j], rl_recv.at[g, j], device_id=right, device_id_type=MESH)

    def sum_left(g, j):
        return pltpu.make_async_remote_copy(
            rr.at[g, j], rr.at[g, j], rr_send.at[g, j], rr_recv.at[g, j], device_id=left, device_id_type=MESH)

    def hand_on(r):
        return pltpu.make_async_remote_copy(
            ubuf.at[r], wbuf.at[m + r, p], n_send.at[r], n_recv.at[r], device_id=following, device_id_type=MESH)

    def w_start(g):
        @when(g >= m)
        def _():
            @when(has_prev)
            def _():
                hand_on(g - m).wait_recv()

            @when(jnp.logical_not(has_prev))
            def _():
                wbuf[g, p] = fresh_buf[:, rows(g - m)]

        @when(has_right)
        def _():
            w_right(g, p).start()

        @when(has_left)
        def _():
            w_left(g, p).start()

    def w_hop(g, h):
        @when(p >= h)
        def _():
            w_right(g, p - h).wait_recv()

            @when(has_right)
            def _():
                w_right(g, p - h).start()

        @when(p + h < n)
        def _():
            w_left(g, p + h).wait_recv()

            @when(has_left)
            def _():
                w_left(g, p + h).start()

    def sum_hop(g, h):
        own = part.at[lax.rem(g, part.shape[0])]

        @when(p == h)
        def _():
            for j in range(n - 1, h, -1):
                value = own[j]
                if h > 0:
                    sum_right(g, j).wait_recv()
                    value = value + rl[g, j].astype(jnp.float32)
                rl[g, j] = value.astype(jnp.bfloat16)
                sum_right(g, j).start()

        @when(p == n - 1 - h)
        def _():
            for j in range(n - 1 - h):
                value = own[j]
                if h > 0:
                    sum_left(g, j).wait_recv()
                    value = value + rr[g, j].astype(jnp.float32)
                rr[g, j] = value.astype(jnp.bfloat16)
                sum_left(g, j).start()

    def update(g):
        for there, edge, buf, arrival in (
            (has_left, p == 0, rl, sum_right),
            (has_right, p == n - 1, rr, sum_left),
        ):
            @when(there)
            def _():
                arrival(g, p).wait_recv()

            @when(edge)
            def _():
                buf[g, p] = jnp.zeros(buf.shape[2:], buf.dtype)
        gradient = part[lax.rem(g, part.shape[0]), p] + rl[g, p].astype(jnp.float32) + rr[g, p].astype(jnp.float32)
        old = wbuf[g, p].astype(jnp.float32)
        stepped = old - gradient
        old_norm = jnp.sqrt(jnp.sum(old * old, axis=-1, keepdims=True))
        new_norm = jnp.sqrt(jnp.sum(stepped * stepped, axis=-1, keepdims=True) + 1e-06)
        new = (stepped * (old_norm / new_norm)).astype(jnp.bfloat16)

        @when(g < m)
        def _():
            ubuf[g] = new

            @when(has_next)
            def _():
                hand_on(g).start()

        @when(g >= m)
        def _():
            leaving[:, rows(g - m)] = new

    def key_part(g):
        t = lax.div(g, m)
        keys, scaled = xbuf[t, 1], xbuf[t, 2]
        w_gu = wbuf[g, :, 0:2].reshape(2 * units, width)
        w_d = wbuf[g, :, 2].reshape(units, width)
        pre = dot(w_gu, keys, NT).reshape(n, 2, block, -1)
        gate, up = pre[:, 0], pre[:, 1]
        d_hidden = dot(w_d, scaled, NT).reshape(gate.shape)
        sig = 1.0 / (1.0 + jnp.exp(-gate))
        act = gate * sig
        hidden = (act * up).astype(jnp.bfloat16).reshape(units, -1)
        d_gate = (d_hidden * up * (sig * (1.0 + gate * (1.0 - sig)))).astype(jnp.bfloat16)
        d_up = (d_hidden * act).astype(jnp.bfloat16)
        d_gu = jnp.stack([d_gate, d_up], axis=1).reshape(2 * units, -1)
        place = lax.rem(g, part.shape[0])
        part[place, :, 0:2] = dot(d_gu, keys, NN).reshape(n, 2, block, width)
        part[place, :, 2] = dot(hidden, scaled, NN).reshape(n, block, width)

    def query_part(g):
        t = lax.div(g, m)
        r = lax.rem(g, m)

        def of(c):
            return [wbuf[g - k, :, c].reshape(units, width) for k in range(group)]

        count = group * units
        pre = dot(xbuf[t, 0], jnp.concatenate(of(0) + of(1), axis=0), NT)
        gate, up = pre[:, :count], pre[:, count:]
        hidden = (gate / (1.0 + jnp.exp(-gate)) * up).astype(jnp.bfloat16)
        out = dot(hidden, jnp.concatenate(of(2), axis=0), NN)

        @when(r == group - 1)
        def _():
            acc[...] = out

        @when(r > group - 1)
        def _():
            acc[...] += out

        @when(r == m - 1)
        def _():
            @when(t == 0)
            def _():
                out_first[...] = acc[...].astype(jnp.bfloat16)

            @when(t == 1)
            def _():
                out_second[...] = acc[...].astype(jnp.bfloat16)

    def thirds(hops):
        size = -(-len(hops) // 3)
        return hops[:size], hops[size:2 * size], hops[2 * size:]

    w_hops = thirds(range(1, n))
    s_hops = thirds(range(1, n - 1))

    w_start(0)

    def slot(step, carry):
        i = step - 2

        @when(valid(i + 3))
        def _():
            w_start(index(i + 3))

        for ahead, hops in zip((2, 1, 0), w_hops):
            @when(valid(i + ahead))
            def _():
                for h in hops:
                    w_hop(index(i + ahead), h)

        for behind, hops in zip((1, 2, 3), s_hops):
            @when(valid(i - behind))
            def _():
                for h in hops:
                    sum_hop(index(i - behind), h)

        @when(valid(i - 3))
        def _():
            update(index(i - 3))

        @when(valid(i))
        def _():
            for t in range(2):
                @when(i == t * period)
                def _():
                    load_x(t).wait()
                    rates = (rates_first, rates_second)[t][...]
                    column = jnp.broadcast_to(rates, (8, rates.shape[1])).T[:, 0:1]
                    xbuf[t, 2] = (-column * xbuf[t, 2].astype(jnp.float32)).astype(jnp.bfloat16)
            key_part(index(i))
            sum_hop(index(i), 0)

        @when(jnp.logical_and(valid(i - 1), lax.rem(lax.rem(i - 1 + period, period), group) == group - 1))
        def _():
            query_part(index(i - 1))

        return carry

    lax.fori_loop(0, rounds + 5, slot, 0)

    def drain(g, carry):
        for j in range(n):
            @when(jnp.logical_and(j <= p, has_right))
            def _():
                w_right(g, j).wait_send()

            @when(jnp.logical_and(j >= p, has_left))
            def _():
                w_left(g, j).wait_send()

            @when(j > p)
            def _():
                sum_right(g, j).wait_send()

            @when(j < p)
            def _():
                sum_left(g, j).wait_send()

        @when(jnp.logical_and(g < m, has_next))
        def _():
            hand_on(g).wait_send()

        return carry

    lax.fori_loop(0, 2 * m, drain, 0)


def on_device(n, nseq, entering, fresh, qkv_first, qkv_second, rates_first, rates_second):
    rows, _, width = fresh.shape
    tokens = qkv_first.shape[1]
    m = min(8, rows // 16)
    period = max(m, 8)
    block = rows // m

    bf16, f32 = jnp.bfloat16, jnp.float32
    vmem = pl.BlockSpec(memory_space=pltpu.VMEM)
    anywhere = pl.BlockSpec(memory_space=pl.ANY)
    rounds = 2 * m
    chunk = (3, block, width)
    dma = pltpu.SemaphoreType.DMA
    out_first, out_second, leaving = pl.pallas_call(
        functools.partial(kernel, n, nseq, m, period),
        out_shape=(
            jax.ShapeDtypeStruct((tokens, width), bf16),
            jax.ShapeDtypeStruct((tokens, width), bf16),
            jax.ShapeDtypeStruct((3, rows, width), bf16),
        ),
        in_specs=[anywhere] * 4 + [vmem, vmem],
        out_specs=(vmem, vmem, vmem),
        scratch_shapes=[
            pltpu.VMEM((rounds, n) + chunk, bf16),
            pltpu.VMEM((rounds, n) + chunk, bf16),
            pltpu.VMEM((rounds, n) + chunk, bf16),
            pltpu.VMEM((4, n) + chunk, f32),
            pltpu.VMEM((2, 3, tokens, width), bf16),
            pltpu.VMEM((tokens, width), f32),
            pltpu.VMEM((m,) + chunk, bf16),
            pltpu.VMEM((3, rows, width), bf16),
            dma((2,)),
            dma((m,)),
            dma(()),
        ] + [dma((rounds, n))] * 7 + [dma((m,)), dma((m,))],
        compiler_params=pltpu.CompilerParams(
            collective_id=0, has_side_effects=True, vmem_limit_bytes=60 * 1024 * 1024),
    )(
        entering[0].transpose(1, 0, 2), fresh.transpose(1, 0, 2),
        qkv_first[0].transpose(1, 0, 2), qkv_second[0].transpose(1, 0, 2), rates_first, rates_second,
    )
    leaving = leaving.transpose(1, 0, 2)
    return (out_first[None], out_second[None], leaving[None])


def solution(mesh):
    placed = (
        P("seq", "tok", None, None),
        P("tok", None, None),
        P("seq", "tok", None, None),
        P("seq", "tok", None, None),
        P("seq", "tok"),
        P("seq", "tok"),
    )
    return jax.shard_map(
        functools.partial(on_device, mesh.shape["tok"], mesh.shape["seq"]),
        mesh=mesh,
        in_specs=placed,
        out_specs=(P("seq", "tok", None), P("seq", "tok", None), P("seq", "tok", None, None)),
        check_vma=False,
    )
```

```python
import functools
import jax
import jax.numpy as jnp
from jax import lax
from jax.experimental import pallas as pl
from jax.experimental.pallas import tpu as pltpu
from jax.sharding import PartitionSpec as P

MESH = pl.DeviceIdType.MESH
NN = (((1,), (0,)), ((), ()))


def dot(a, b, dims):
    return lax.dot_general(a, b, dims, preferred_element_type=jnp.float32)


def kernel(
    n, nseq, m, period,
    ent, fresh, x_first, x_second, rates_first, rates_second,
    out_first, out_second, leaving,
    wbuf, rl, rr, part, xbuf, flipped, acc, ubuf,
    fresh_buf, rates, rates_sem, x_sem, own_sem, fresh_sem, w_recv, w_send_r, w_send_l, rl_recv, rl_send, rr_recv, rr_send, n_send, n_recv,
):
    rounds = 2 * period
    s = lax.axis_index("seq")
    p = lax.axis_index("tok")
    when = pl.when
    has_left, has_right = p > 0, p < n - 1
    has_prev, has_next = s > 0, s < nseq - 1
    left, right = (s, jnp.maximum(p - 1, 0)), (s, jnp.minimum(p + 1, n - 1))
    prev, following = (jnp.maximum(s - 1, 0), p), (jnp.minimum(s + 1, nseq - 1), p)
    block, width = wbuf.shape[3:]
    units = n * block
    group = 2 if m % 2 == 0 else 1

    def rows(r):
        return pl.ds(pl.multiple_of(r * block, block), block)

    def load_x(t):
        src = x_first if t == 0 else x_second
        return pltpu.make_async_copy(src, xbuf.at[t], x_sem.at[t])

    def load_rates(t):
        return pltpu.make_async_copy((rates_first, rates_second)[t], rates.at[t], rates_sem.at[t])

    def load_own(r):
        return pltpu.make_async_copy(ent.at[:, r * block:(r + 1) * block], wbuf.at[r, p], own_sem.at[r])

    load_fresh = pltpu.make_async_copy(fresh, fresh_buf, fresh_sem)

    for r in range(m):
        load_own(r).start()
    for t in range(2):
        load_x(t).start()
        load_rates(t).start()
    load_fresh.start()

    barrier = pltpu.get_barrier_semaphore()
    for there, device in ((has_left, left), (has_right, right), (has_prev, prev), (has_next, following)):
        @when(there)
        def _():
            pl.semaphore_signal(barrier, inc=1, device_id=device, device_id_type=MESH)
    for r in range(m):
        load_own(r).wait()
    load_fresh.wait()
    peers = sum(jnp.where(there, 1, 0) for there in (has_left, has_right, has_prev, has_next))
    pl.semaphore_wait(barrier, peers)

    def valid(i):
        return jnp.logical_and(jnp.logical_and(i >= 0, i < rounds), lax.rem(i + period, period) < m)

    def index(i):
        return lax.div(i, period) * m + lax.rem(i, period)

    def w_right(g, j):
        return pltpu.make_async_remote_copy(
            wbuf.at[g, j], wbuf.at[g, j], w_send_r.at[g, j], w_recv.at[g, j], device_id=right, device_id_type=MESH)

    def w_left(g, j):
        return pltpu.make_async_remote_copy(
            wbuf.at[g, j], wbuf.at[g, j], w_send_l.at[g, j], w_recv.at[g, j], device_id=left, device_id_type=MESH)

    def sum_right(g, j):
        return pltpu.make_async_remote_copy(
            rl.at[g, j], rl.at[g, j], rl_send.at[g, j], rl_recv.at[g, j], device_id=right, device_id_type=MESH)

    def sum_left(g, j):
        return pltpu.make_async_remote_copy(
            rr.at[g, j], rr.at[g, j], rr_send.at[g, j], rr_recv.at[g, j], device_id=left, device_id_type=MESH)

    def hand_on(r):
        return pltpu.make_async_remote_copy(
            ubuf.at[r], wbuf.at[m + r, p], n_send.at[r], n_recv.at[r], device_id=following, device_id_type=MESH)

    def w_start(g):
        @when(g >= m)
        def _():
            @when(has_prev)
            def _():
                hand_on(g - m).wait_recv()

            @when(jnp.logical_not(has_prev))
            def _():
                wbuf[g, p] = fresh_buf[:, rows(g - m)]

        @when(has_right)
        def _():
            w_right(g, p).start()

        @when(has_left)
        def _():
            w_left(g, p).start()

    def w_hop(g, h):
        @when(p >= h)
        def _():
            w_right(g, p - h).wait_recv()

            @when(has_right)
            def _():
                w_right(g, p - h).start()

        @when(p + h < n)
        def _():
            w_left(g, p + h).wait_recv()

            @when(has_left)
            def _():
                w_left(g, p + h).start()

    def sum_hop(g, h):
        own = part.at[lax.rem(g, part.shape[0])]

        @when(p == h)
        def _():
            for j in range(n - 1, h, -1):
                value = own[j]
                if h > 0:
                    sum_right(g, j).wait_recv()
                    value = value + rl[g, j].astype(jnp.float32)
                rl[g, j] = value.astype(jnp.bfloat16)
                sum_right(g, j).start()

        @when(p == n - 1 - h)
        def _():
            for j in range(n - 1 - h):
                value = own[j]
                if h > 0:
                    sum_left(g, j).wait_recv()
                    value = value + rr[g, j].astype(jnp.float32)
                rr[g, j] = value.astype(jnp.bfloat16)
                sum_left(g, j).start()

    def update(g):
        for there, edge, buf, arrival in (
            (has_left, p == 0, rl, sum_right),
            (has_right, p == n - 1, rr, sum_left),
        ):
            @when(there)
            def _():
                arrival(g, p).wait_recv()

            @when(edge)
            def _():
                buf[g, p] = jnp.zeros(buf.shape[2:], buf.dtype)
        gradient = part[lax.rem(g, part.shape[0]), p] + rl[g, p].astype(jnp.float32) + rr[g, p].astype(jnp.float32)
        old = wbuf[g, p].astype(jnp.float32)
        stepped = old - gradient
        old_norm = jnp.sqrt(jnp.sum(old * old, axis=-1, keepdims=True))
        new_norm = jnp.sqrt(jnp.sum(stepped * stepped, axis=-1, keepdims=True) + 1e-06)
        new = (stepped * (old_norm / new_norm)).astype(jnp.bfloat16)

        @when(g < m)
        def _():
            ubuf[g] = new

            @when(has_next)
            def _():
                hand_on(g).start()

        @when(g >= m)
        def _():
            leaving[:, rows(g - m)] = new

    def prepare(t):
        load_x(t).wait()
        load_rates(t).wait()
        column = jnp.broadcast_to(rates[t], (8, rates.shape[2])).T[:, 0:1]
        xbuf[t, 2] = (-column * xbuf[t, 2].astype(jnp.float32)).astype(jnp.bfloat16)
        for c in range(3):
            flipped[t, c] = xbuf[t, c].T

    def key_part(g):
        t = lax.div(g, m)
        keys, scaled = xbuf[t, 1], xbuf[t, 2]
        w_gu = wbuf[g, :, 0:2].reshape(2 * units, width)
        w_d = wbuf[g, :, 2].reshape(units, width)
        pre = dot(w_gu, flipped[t, 1], NN).reshape(n, 2, block, -1)
        gate, up = pre[:, 0], pre[:, 1]
        d_hidden = dot(w_d, flipped[t, 2], NN).reshape(gate.shape)
        sig = 1.0 / (1.0 + jnp.exp(-gate))
        act = gate * sig
        hidden = (act * up).astype(jnp.bfloat16).reshape(units, -1)
        d_gate = (d_hidden * up * (sig * (1.0 + gate * (1.0 - sig)))).astype(jnp.bfloat16)
        d_up = (d_hidden * act).astype(jnp.bfloat16)
        d_gu = jnp.stack([d_gate, d_up], axis=1).reshape(2 * units, -1)
        place = lax.rem(g, part.shape[0])
        part[place, :, 0:2] = dot(d_gu, keys, NN).reshape(n, 2, block, width)
        part[place, :, 2] = dot(hidden, scaled, NN).reshape(n, block, width)

    def query_part(g):
        t = lax.div(g, m)
        r = lax.rem(g, m)

        def of(c):
            return [wbuf[g - k, :, c].reshape(units, width) for k in range(group)]

        count = group * units
        pre = dot(jnp.concatenate(of(0) + of(1), axis=0), flipped[t, 0], NN)
        gate, up = pre[:count], pre[count:]
        hidden = (gate / (1.0 + jnp.exp(-gate)) * up).astype(jnp.bfloat16)
        out = dot(hidden.T, jnp.concatenate(of(2), axis=0), NN)

        @when(r == group - 1)
        def _():
            acc[...] = out

        @when(r > group - 1)
        def _():
            acc[...] += out

        @when(r == m - 1)
        def _():
            @when(t == 0)
            def _():
                out_first[...] = acc[...].astype(jnp.bfloat16)

            @when(t == 1)
            def _():
                out_second[...] = acc[...].astype(jnp.bfloat16)

    def thirds(hops):
        size = -(-len(hops) // 3)
        return hops[:size], hops[size:2 * size], hops[2 * size:]

    w_hops = thirds(range(1, n))
    s_hops = thirds(range(1, n - 1))

    w_start(0)

    def slot(step, carry):
        i = step - 2

        @when(valid(i + 3))
        def _():
            w_start(index(i + 3))

        for ahead, hops in zip((2, 1, 0), w_hops):
            @when(valid(i + ahead))
            def _():
                for h in hops:
                    w_hop(index(i + ahead), h)

        for t in range(2):
            @when(i == t - 2)
            def _():
                prepare(t)

        for behind, hops in zip((1, 2, 3), s_hops):
            @when(valid(i - behind))
            def _():
                for h in hops:
                    sum_hop(index(i - behind), h)

        @when(valid(i - 3))
        def _():
            update(index(i - 3))

        @when(valid(i))
        def _():
            key_part(index(i))
            sum_hop(index(i), 0)

        @when(jnp.logical_and(valid(i - 1), lax.rem(lax.rem(i - 1 + period, period), group) == group - 1))
        def _():
            query_part(index(i - 1))

        return carry

    lax.fori_loop(0, rounds + 5, slot, 0)

    def drain(g, carry):
        for j in range(n):
            @when(jnp.logical_and(j <= p, has_right))
            def _():
                w_right(g, j).wait_send()

            @when(jnp.logical_and(j >= p, has_left))
            def _():
                w_left(g, j).wait_send()

            @when(j > p)
            def _():
                sum_right(g, j).wait_send()

            @when(j < p)
            def _():
                sum_left(g, j).wait_send()

        @when(jnp.logical_and(g < m, has_next))
        def _():
            hand_on(g).wait_send()

        return carry

    lax.fori_loop(0, 2 * m, drain, 0)


def on_device(n, nseq, entering, fresh, qkv_first, qkv_second, rates_first, rates_second):
    rows, _, width = fresh.shape
    tokens = qkv_first.shape[1]
    m = min(8, rows // 16)
    period = max(m, 8)
    block = rows // m

    operands = [a.transpose(1, 0, 2) for a in (entering[0], fresh, qkv_first[0], qkv_second[0])]
    operands += [rates_first, rates_second]
    bf16, f32 = jnp.bfloat16, jnp.float32
    vmem = pl.BlockSpec(memory_space=pltpu.VMEM)
    hbm = pl.BlockSpec(memory_space=pltpu.HBM)
    rounds = 2 * m
    chunk = (3, block, width)
    dma = pltpu.SemaphoreType.DMA
    out_first, out_second, leaving = pl.pallas_call(
        functools.partial(kernel, n, nseq, m, period),
        out_shape=(
            jax.ShapeDtypeStruct((tokens, width), bf16),
            jax.ShapeDtypeStruct((tokens, width), bf16),
            jax.ShapeDtypeStruct((3, rows, width), bf16),
        ),
        in_specs=[hbm] * 6,
        out_specs=(vmem, vmem, vmem),
        scratch_shapes=[
            pltpu.VMEM((rounds, n) + chunk, bf16),
            pltpu.VMEM((rounds, n) + chunk, bf16),
            pltpu.VMEM((rounds, n) + chunk, bf16),
            pltpu.VMEM((4, n) + chunk, f32),
            pltpu.VMEM((2, 3, tokens, width), bf16),
            pltpu.VMEM((2, 3, width, tokens), bf16),
            pltpu.VMEM((tokens, width), f32),
            pltpu.VMEM((m,) + chunk, bf16),
            pltpu.VMEM((3, rows, width), bf16),
            pltpu.VMEM((2, 1, tokens), f32),
            dma((2,)),
            dma((2,)),
            dma((m,)),
            dma(()),
        ] + [dma((rounds, n))] * 7 + [dma((m,)), dma((m,))],
        compiler_params=pltpu.CompilerParams(
            collective_id=0, has_side_effects=True, vmem_limit_bytes=48 * 1024 * 1024),
    )(
        *(pltpu.with_memory_space_constraint(operand, pltpu.HBM) for operand in operands)
    )
    leaving = leaving.transpose(1, 0, 2)
    return (out_first[None], out_second[None], leaving[None])


def solution(mesh):
    placed = (
        P("seq", "tok", None, None),
        P("tok", None, None),
        P("seq", "tok", None, None),
        P("seq", "tok", None, None),
        P("seq", "tok"),
        P("seq", "tok"),
    )
    return jax.shard_map(
        functools.partial(on_device, mesh.shape["tok"], mesh.shape["seq"]),
        mesh=mesh,
        in_specs=placed,
        out_specs=(P("seq", "tok", None), P("seq", "tok", None), P("seq", "tok", None, None)),
        check_vma=False,
    )
```

```python
import functools
import jax
import jax.numpy as jnp
from jax import lax
from jax.experimental import pallas as pl
from jax.experimental.pallas import tpu as pltpu
from jax.sharding import PartitionSpec as P

MESH = pl.DeviceIdType.MESH
NN = (((1,), (0,)), ((), ()))


def dot(a, b, dims):
    return lax.dot_general(a, b, dims, preferred_element_type=jnp.float32)


def kernel(
    n, nseq, m, period,
    ent, fresh, x_first, x_second, rates_first, rates_second,
    out_first, out_second, leaving,
    wbuf, rl, rr, part, xbuf, flipped, acc, ubuf,
    fresh_buf, rates, rates_sem, x_sem, own_sem, fresh_sem, w_recv, w_send_r, w_send_l, rl_recv, rl_send, rr_recv, rr_send, n_send, n_recv,
):
    rounds = 2 * period
    s = lax.axis_index("seq")
    p = lax.axis_index("tok")
    when = pl.when
    has_left, has_right = p > 0, p < n - 1
    has_prev, has_next = s > 0, s < nseq - 1
    left, right = (s, jnp.maximum(p - 1, 0)), (s, jnp.minimum(p + 1, n - 1))
    prev, following = (jnp.maximum(s - 1, 0), p), (jnp.minimum(s + 1, nseq - 1), p)
    block, width = wbuf.shape[3:]
    units = n * block
    group = 2 if m % 2 == 0 else 1

    def rows(r):
        return pl.ds(pl.multiple_of(r * block, block), block)

    def load_x(t):
        src = x_first if t == 0 else x_second
        return pltpu.make_async_copy(src, xbuf.at[t], x_sem.at[t])

    def load_rates(t):
        return pltpu.make_async_copy((rates_first, rates_second)[t], rates.at[t], rates_sem.at[t])

    def load_own(r):
        return pltpu.make_async_copy(ent.at[:, r * block:(r + 1) * block], wbuf.at[r, p], own_sem.at[r])

    load_fresh = pltpu.make_async_copy(fresh, fresh_buf, fresh_sem)

    for r in range(m):
        load_own(r).start()

    barrier = pltpu.get_barrier_semaphore()
    for there, device in ((has_left, left), (has_right, right), (has_prev, prev), (has_next, following)):
        @when(there)
        def _():
            pl.semaphore_signal(barrier, inc=1, device_id=device, device_id_type=MESH)
    load_own(0).wait()
    peers = sum(jnp.where(there, 1, 0) for there in (has_left, has_right, has_prev, has_next))
    pl.semaphore_wait(barrier, peers)

    def valid(i):
        return jnp.logical_and(jnp.logical_and(i >= 0, i < rounds), lax.rem(i + period, period) < m)

    def index(i):
        return lax.div(i, period) * m + lax.rem(i, period)

    def w_right(g, j):
        return pltpu.make_async_remote_copy(
            wbuf.at[g, j], wbuf.at[g, j], w_send_r.at[g, j], w_recv.at[g, j], device_id=right, device_id_type=MESH)

    def w_left(g, j):
        return pltpu.make_async_remote_copy(
            wbuf.at[g, j], wbuf.at[g, j], w_send_l.at[g, j], w_recv.at[g, j], device_id=left, device_id_type=MESH)

    def sum_right(g, j):
        return pltpu.make_async_remote_copy(
            rl.at[g, j], rl.at[g, j], rl_send.at[g, j], rl_recv.at[g, j], device_id=right, device_id_type=MESH)

    def sum_left(g, j):
        return pltpu.make_async_remote_copy(
            rr.at[g, j], rr.at[g, j], rr_send.at[g, j], rr_recv.at[g, j], device_id=left, device_id_type=MESH)

    def hand_on(r):
        return pltpu.make_async_remote_copy(
            ubuf.at[r], wbuf.at[m + r, p], n_send.at[r], n_recv.at[r], device_id=following, device_id_type=MESH)

    def w_start(g):
        @when(g >= m)
        def _():
            @when(has_prev)
            def _():
                hand_on(g - m).wait_recv()

            @when(jnp.logical_not(has_prev))
            def _():
                wbuf[g, p] = fresh_buf[:, rows(g - m)]

        @when(has_right)
        def _():
            w_right(g, p).start()

        @when(has_left)
        def _():
            w_left(g, p).start()

    def w_hop(g, h):
        @when(p >= h)
        def _():
            w_right(g, p - h).wait_recv()

            @when(has_right)
            def _():
                w_right(g, p - h).start()

        @when(p + h < n)
        def _():
            w_left(g, p + h).wait_recv()

            @when(has_left)
            def _():
                w_left(g, p + h).start()

    def sum_hop(g, h):
        own = part.at[lax.rem(g, part.shape[0])]

        @when(p == h)
        def _():
            for j in range(n - 1, h, -1):
                value = own[j]
                if h > 0:
                    sum_right(g, j).wait_recv()
                    value = value + rl[g, j].astype(jnp.float32)
                rl[g, j] = value.astype(jnp.bfloat16)
                sum_right(g, j).start()

        @when(p == n - 1 - h)
        def _():
            for j in range(n - 1 - h):
                value = own[j]
                if h > 0:
                    sum_left(g, j).wait_recv()
                    value = value + rr[g, j].astype(jnp.float32)
                rr[g, j] = value.astype(jnp.bfloat16)
                sum_left(g, j).start()

    def update(g):
        for there, edge, buf, arrival in (
            (has_left, p == 0, rl, sum_right),
            (has_right, p == n - 1, rr, sum_left),
        ):
            @when(there)
            def _():
                arrival(g, p).wait_recv()

            @when(edge)
            def _():
                buf[g, p] = jnp.zeros(buf.shape[2:], buf.dtype)
        gradient = part[lax.rem(g, part.shape[0]), p] + rl[g, p].astype(jnp.float32) + rr[g, p].astype(jnp.float32)
        old = wbuf[g, p].astype(jnp.float32)
        stepped = old - gradient
        old_norm = jnp.sqrt(jnp.sum(old * old, axis=-1, keepdims=True))
        new_norm = jnp.sqrt(jnp.sum(stepped * stepped, axis=-1, keepdims=True) + 1e-06)
        new = (stepped * (old_norm / new_norm)).astype(jnp.bfloat16)

        @when(g < m)
        def _():
            ubuf[g] = new

            @when(has_next)
            def _():
                hand_on(g).start()

        @when(g >= m)
        def _():
            leaving[:, rows(g - m)] = new

    def prepare(t):
        load_x(t).wait()
        load_rates(t).wait()
        column = jnp.broadcast_to(rates[t], (8, rates.shape[2])).T[:, 0:1]
        xbuf[t, 2] = (-column * xbuf[t, 2].astype(jnp.float32)).astype(jnp.bfloat16)
        for c in range(3):
            flipped[t, c] = xbuf[t, c].T

    def key_part(g):
        t = lax.div(g, m)
        keys, scaled = xbuf[t, 1], xbuf[t, 2]
        w_gu = wbuf[g, :, 0:2].reshape(2 * units, width)
        w_d = wbuf[g, :, 2].reshape(units, width)
        pre = dot(w_gu, flipped[t, 1], NN).reshape(n, 2, block, -1)
        gate, up = pre[:, 0], pre[:, 1]
        d_hidden = dot(w_d, flipped[t, 2], NN).reshape(gate.shape)
        sig = 1.0 / (1.0 + jnp.exp(-gate))
        act = gate * sig
        hidden = (act * up).astype(jnp.bfloat16).reshape(units, -1)
        d_gate = (d_hidden * up * (sig * (1.0 + gate * (1.0 - sig)))).astype(jnp.bfloat16)
        d_up = (d_hidden * act).astype(jnp.bfloat16)
        d_gu = jnp.stack([d_gate, d_up], axis=1).reshape(2 * units, -1)
        place = lax.rem(g, part.shape[0])
        part[place, :, 0:2] = dot(d_gu, keys, NN).reshape(n, 2, block, width)
        part[place, :, 2] = dot(hidden, scaled, NN).reshape(n, block, width)

    def query_part(g):
        t = lax.div(g, m)
        r = lax.rem(g, m)

        def of(c):
            return [wbuf[g - k, :, c].reshape(units, width) for k in range(group)]

        count = group * units
        pre = dot(jnp.concatenate(of(0) + of(1), axis=0), flipped[t, 0], NN)
        gate, up = pre[:count], pre[count:]
        hidden = (gate / (1.0 + jnp.exp(-gate)) * up).astype(jnp.bfloat16)
        out = dot(hidden.T, jnp.concatenate(of(2), axis=0), NN)

        @when(r == group - 1)
        def _():
            acc[...] = out

        @when(r > group - 1)
        def _():
            acc[...] += out

        @when(r == m - 1)
        def _():
            @when(t == 0)
            def _():
                out_first[...] = acc[...].astype(jnp.bfloat16)

            @when(t == 1)
            def _():
                out_second[...] = acc[...].astype(jnp.bfloat16)

    def thirds(hops):
        size = -(-len(hops) // 3)
        return hops[:size], hops[size:2 * size], hops[2 * size:]

    w_hops = thirds(range(1, n))
    s_hops = thirds(range(1, n - 1))

    w_start(0)
    for t in range(2):
        load_x(t).start()
        load_rates(t).start()
    load_fresh.start()
    for r in range(1, m):
        load_own(r).wait()

    def slot(step, carry):
        i = step - 2

        @when(valid(i + 3))
        def _():
            w_start(index(i + 3))

        for ahead, hops in zip((2, 1, 0), w_hops):
            @when(valid(i + ahead))
            def _():
                for h in hops:
                    w_hop(index(i + ahead), h)

        for t in range(2):
            @when(i == t - 2)
            def _():
                prepare(t)
                if t == 1:
                    load_fresh.wait()

        for behind, hops in zip((2, 3, 4), s_hops):
            @when(valid(i - behind))
            def _():
                for h in hops:
                    sum_hop(index(i - behind), h)

        @when(valid(i - 4))
        def _():
            update(index(i - 4))

        @when(valid(i))
        def _():
            key_part(index(i))
            sum_hop(index(i), 0)

        @when(jnp.logical_and(valid(i - 1), lax.rem(lax.rem(i - 1 + period, period), group) == group - 1))
        def _():
            query_part(index(i - 1))

        return carry

    lax.fori_loop(0, rounds + 6, slot, 0)

    def drain(g, carry):
        for j in range(n):
            @when(jnp.logical_and(j <= p, has_right))
            def _():
                w_right(g, j).wait_send()

            @when(jnp.logical_and(j >= p, has_left))
            def _():
                w_left(g, j).wait_send()

            @when(j > p)
            def _():
                sum_right(g, j).wait_send()

            @when(j < p)
            def _():
                sum_left(g, j).wait_send()

        @when(jnp.logical_and(g < m, has_next))
        def _():
            hand_on(g).wait_send()

        return carry

    lax.fori_loop(0, 2 * m, drain, 0)


def on_device(n, nseq, entering, fresh, qkv_first, qkv_second, rates_first, rates_second):
    rows, _, width = fresh.shape
    tokens = qkv_first.shape[1]
    m = min(8, rows // 16)
    period = max(m, 8)
    block = rows // m

    operands = [a.transpose(1, 0, 2) for a in (entering[0], fresh, qkv_first[0], qkv_second[0])]
    operands += [rates_first, rates_second]
    bf16, f32 = jnp.bfloat16, jnp.float32
    vmem = pl.BlockSpec(memory_space=pltpu.VMEM)
    hbm = pl.BlockSpec(memory_space=pltpu.HBM)
    rounds = 2 * m
    chunk = (3, block, width)
    dma = pltpu.SemaphoreType.DMA
    out_first, out_second, leaving = pl.pallas_call(
        functools.partial(kernel, n, nseq, m, period),
        out_shape=(
            jax.ShapeDtypeStruct((tokens, width), bf16),
            jax.ShapeDtypeStruct((tokens, width), bf16),
            jax.ShapeDtypeStruct((3, rows, width), bf16),
        ),
        in_specs=[hbm] * 6,
        out_specs=(vmem, vmem, vmem),
        scratch_shapes=[
            pltpu.VMEM((rounds, n) + chunk, bf16),
            pltpu.VMEM((rounds, n) + chunk, bf16),
            pltpu.VMEM((rounds, n) + chunk, bf16),
            pltpu.VMEM((4, n) + chunk, f32),
            pltpu.VMEM((2, 3, tokens, width), bf16),
            pltpu.VMEM((2, 3, width, tokens), bf16),
            pltpu.VMEM((tokens, width), f32),
            pltpu.VMEM((m,) + chunk, bf16),
            pltpu.VMEM((3, rows, width), bf16),
            pltpu.VMEM((2, 1, tokens), f32),
            dma((2,)),
            dma((2,)),
            dma((m,)),
            dma(()),
        ] + [dma((rounds, n))] * 7 + [dma((m,)), dma((m,))],
        compiler_params=pltpu.CompilerParams(
            collective_id=0, has_side_effects=True, vmem_limit_bytes=48 * 1024 * 1024),
    )(
        *(pltpu.with_memory_space_constraint(operand, pltpu.HBM) for operand in operands)
    )
    leaving = leaving.transpose(1, 0, 2)
    return (out_first[None], out_second[None], leaving[None])


def solution(mesh):
    placed = (
        P("seq", "tok", None, None),
        P("tok", None, None),
        P("seq", "tok", None, None),
        P("seq", "tok", None, None),
        P("seq", "tok"),
        P("seq", "tok"),
    )
    return jax.shard_map(
        functools.partial(on_device, mesh.shape["tok"], mesh.shape["seq"]),
        mesh=mesh,
        in_specs=placed,
        out_specs=(P("seq", "tok", None), P("seq", "tok", None), P("seq", "tok", None, None)),
        check_vma=False,
    )
```

```python
import functools
import jax
import jax.numpy as jnp
from jax import lax
from jax.experimental import pallas as pl
from jax.experimental.pallas import tpu as pltpu
from jax.sharding import PartitionSpec as P

MESH = pl.DeviceIdType.MESH
NN = (((1,), (0,)), ((), ()))


def dot(a, b, dims):
    return lax.dot_general(a, b, dims, preferred_element_type=jnp.float32)


def kernel(
    n, nseq, m, period,
    ent, fresh, x_first, x_second, rates_first, rates_second,
    out_first, out_second, leaving,
    wbuf, rl, rr, part, xbuf, flipped, acc, ubuf,
    fresh_buf, rates, rates_sem, x_sem, own_sem, fresh_sem, w_recv, w_send_r, w_send_l, rl_recv, rl_send, rr_recv, rr_send, n_send, n_recv,
):
    rounds = 2 * period
    s = lax.axis_index("seq")
    p = lax.axis_index("tok")
    when = pl.when
    has_left, has_right = p > 0, p < n - 1
    has_prev, has_next = s > 0, s < nseq - 1
    left, right = (s, jnp.maximum(p - 1, 0)), (s, jnp.minimum(p + 1, n - 1))
    prev, following = (jnp.maximum(s - 1, 0), p), (jnp.minimum(s + 1, nseq - 1), p)
    block, width = wbuf.shape[3:]
    units = n * block
    group = 2 if m % 2 == 0 else 1

    def rows(r):
        return pl.ds(pl.multiple_of(r * block, block), block)

    def load_x(t):
        src = x_first if t == 0 else x_second
        return pltpu.make_async_copy(src, xbuf.at[t], x_sem.at[t])

    def load_rates(t):
        return pltpu.make_async_copy((rates_first, rates_second)[t], rates.at[t], rates_sem.at[t])

    def load_own(r):
        return pltpu.make_async_copy(ent.at[:, r * block:(r + 1) * block], wbuf.at[r, p], own_sem.at[r])

    load_fresh = pltpu.make_async_copy(fresh, fresh_buf, fresh_sem)

    for r in range(m):
        load_own(r).start()

    barrier = pltpu.get_barrier_semaphore()
    for there, device in ((has_left, left), (has_right, right), (has_prev, prev), (has_next, following)):
        @when(there)
        def _():
            pl.semaphore_signal(barrier, inc=1, device_id=device, device_id_type=MESH)
    peers = sum(jnp.where(there, 1, 0) for there in (has_left, has_right, has_prev, has_next))
    pl.semaphore_wait(barrier, peers)

    def valid(i):
        return jnp.logical_and(jnp.logical_and(i >= 0, i < rounds), lax.rem(i + 2 * period, period) < m)

    def in_tick(t, i):
        return jnp.logical_and(i >= t * period, i < t * period + m)

    def index(i):
        return lax.div(i, period) * m + lax.rem(i, period)

    def w_right(g, j):
        return pltpu.make_async_remote_copy(
            wbuf.at[g, j], wbuf.at[g, j], w_send_r.at[g, j], w_recv.at[g, j], device_id=right, device_id_type=MESH)

    def w_left(g, j):
        return pltpu.make_async_remote_copy(
            wbuf.at[g, j], wbuf.at[g, j], w_send_l.at[g, j], w_recv.at[g, j], device_id=left, device_id_type=MESH)

    def sum_right(g, j):
        return pltpu.make_async_remote_copy(
            rl.at[g, j], rl.at[g, j], rl_send.at[g, j], rl_recv.at[g, j], device_id=right, device_id_type=MESH)

    def sum_left(g, j):
        return pltpu.make_async_remote_copy(
            rr.at[g, j], rr.at[g, j], rr_send.at[g, j], rr_recv.at[g, j], device_id=left, device_id_type=MESH)

    def hand_on(r):
        return pltpu.make_async_remote_copy(
            ubuf.at[r], wbuf.at[m + r, p], n_send.at[r], n_recv.at[r], device_id=following, device_id_type=MESH)

    def w_start(g):
        @when(g >= m)
        def _():
            @when(has_prev)
            def _():
                hand_on(g - m).wait_recv()

            @when(jnp.logical_not(has_prev))
            def _():
                wbuf[g, p] = fresh_buf[:, rows(g - m)]

        @when(has_right)
        def _():
            w_right(g, p).start()

        @when(has_left)
        def _():
            w_left(g, p).start()

    def w_hop(g, h):
        @when(p >= h)
        def _():
            w_right(g, p - h).wait_recv()

            @when(has_right)
            def _():
                w_right(g, p - h).start()

        @when(p + h < n)
        def _():
            w_left(g, p + h).wait_recv()

            @when(has_left)
            def _():
                w_left(g, p + h).start()

    def sum_hop(g, h):
        own = part.at[lax.rem(g, part.shape[0])]

        @when(p == h)
        def _():
            for j in range(n - 1, h, -1):
                value = own[j]
                if h > 0:
                    sum_right(g, j).wait_recv()
                    value = value + rl[g, j].astype(jnp.float32)
                rl[g, j] = value.astype(jnp.bfloat16)
                sum_right(g, j).start()

        @when(p == n - 1 - h)
        def _():
            for j in range(n - 1 - h):
                value = own[j]
                if h > 0:
                    sum_left(g, j).wait_recv()
                    value = value + rr[g, j].astype(jnp.float32)
                rr[g, j] = value.astype(jnp.bfloat16)
                sum_left(g, j).start()

    def update(g):
        for there, edge, buf, arrival in (
            (has_left, p == 0, rl, sum_right),
            (has_right, p == n - 1, rr, sum_left),
        ):
            @when(there)
            def _():
                arrival(g, p).wait_recv()

            @when(edge)
            def _():
                buf[g, p] = jnp.zeros(buf.shape[2:], buf.dtype)
        gradient = part[lax.rem(g, part.shape[0]), p] + rl[g, p].astype(jnp.float32) + rr[g, p].astype(jnp.float32)
        old = wbuf[g, p].astype(jnp.float32)
        stepped = old - gradient
        old_norm = jnp.sqrt(jnp.sum(old * old, axis=-1, keepdims=True))
        new_norm = jnp.sqrt(jnp.sum(stepped * stepped, axis=-1, keepdims=True) + 1e-06)
        new = (stepped * (old_norm / new_norm)).astype(jnp.bfloat16)

        @when(g < m)
        def _():
            ubuf[g] = new

            @when(has_next)
            def _():
                hand_on(g).start()

        @when(g >= m)
        def _():
            leaving[:, rows(g - m)] = new

    def prepare(t):
        load_x(t).wait()
        load_rates(t).wait()
        column = jnp.broadcast_to(rates[t], (8, rates.shape[2])).T[:, 0:1]
        xbuf[t, 2] = (-column * xbuf[t, 2].astype(jnp.float32)).astype(jnp.bfloat16)
        for c in range(3):
            flipped[t, c] = xbuf[t, c].T

    def key_part(g):
        t = lax.div(g, m)
        keys, scaled = xbuf[t, 1], xbuf[t, 2]
        w_gu = wbuf[g, :, 0:2].reshape(2 * units, width)
        w_d = wbuf[g, :, 2].reshape(units, width)
        pre = dot(w_gu, flipped[t, 1], NN).reshape(n, 2, block, -1)
        gate, up = pre[:, 0], pre[:, 1]
        d_hidden = dot(w_d, flipped[t, 2], NN).reshape(gate.shape)
        sig = 1.0 / (1.0 + jnp.exp(-gate))
        act = gate * sig
        hidden = (act * up).astype(jnp.bfloat16).reshape(units, -1)
        d_gate = (d_hidden * up * (sig * (1.0 + gate * (1.0 - sig)))).astype(jnp.bfloat16)
        d_up = (d_hidden * act).astype(jnp.bfloat16)
        d_gu = jnp.stack([d_gate, d_up], axis=1).reshape(2 * units, -1)
        place = lax.rem(g, part.shape[0])
        part[place, :, 0:2] = dot(d_gu, keys, NN).reshape(n, 2, block, width)
        part[place, :, 2] = dot(hidden, scaled, NN).reshape(n, block, width)

    def query_part(g):
        t = lax.div(g, m)
        r = lax.rem(g, m)

        def of(c):
            return [wbuf[g - k, :, c].reshape(units, width) for k in range(group)]

        count = group * units
        pre = dot(jnp.concatenate(of(0) + of(1), axis=0), flipped[t, 0], NN)
        gate, up = pre[:count], pre[count:]
        hidden = (gate / (1.0 + jnp.exp(-gate)) * up).astype(jnp.bfloat16)
        out = dot(hidden.T, jnp.concatenate(of(2), axis=0), NN)

        @when(r == group - 1)
        def _():
            acc[...] = out

        @when(r > group - 1)
        def _():
            acc[...] += out

        @when(r == m - 1)
        def _():
            @when(t == 0)
            def _():
                out_first[...] = acc[...].astype(jnp.bfloat16)

            @when(t == 1)
            def _():
                out_second[...] = acc[...].astype(jnp.bfloat16)

    def thirds(hops):
        size = -(-len(hops) // 3)
        return hops[:size], hops[size:2 * size], hops[2 * size:]

    leads = ((4, 3, 2, 0), (3, 2, 1, 0))
    w_hops = thirds(range(1, n))
    s_hops = thirds(range(1, n - 1))

    for t in range(2):
        load_x(t).start()
        load_rates(t).start()
    load_fresh.start()
    for r in range(m):
        load_own(r).wait()

    def slot(step, carry):
        i = step - leads[0][0]

        for stage in range(4):
            for t in range(2):
                ahead = leads[t][stage]

                @when(in_tick(t, i + ahead))
                def _():
                    if stage == 0:
                        w_start(index(i + ahead))
                    else:
                        for h in w_hops[stage - 1]:
                            w_hop(index(i + ahead), h)

        for t in range(2):
            @when(i == t - 3)
            def _():
                prepare(t)
                if t == 1:
                    load_fresh.wait()

        for behind, hops in zip((2, 3, 4), s_hops):
            @when(valid(i - behind))
            def _():
                for h in hops:
                    sum_hop(index(i - behind), h)

        @when(valid(i - 4))
        def _():
            update(index(i - 4))

        @when(valid(i))
        def _():
            key_part(index(i))
            sum_hop(index(i), 0)

        @when(jnp.logical_and(valid(i - 1), lax.rem(lax.rem(i - 1 + 2 * period, period), group) == group - 1))
        def _():
            query_part(index(i - 1))

        return carry

    lax.fori_loop(0, rounds + 8, slot, 0)

    def drain(g, carry):
        for j in range(n):
            @when(jnp.logical_and(j <= p, has_right))
            def _():
                w_right(g, j).wait_send()

            @when(jnp.logical_and(j >= p, has_left))
            def _():
                w_left(g, j).wait_send()

            @when(j > p)
            def _():
                sum_right(g, j).wait_send()

            @when(j < p)
            def _():
                sum_left(g, j).wait_send()

        @when(jnp.logical_and(g < m, has_next))
        def _():
            hand_on(g).wait_send()

        return carry

    lax.fori_loop(0, 2 * m, drain, 0)


def store_kernel(a, b, c, a_out, b_out, c_out, sems):
    copies = [
        pltpu.make_async_copy(src, dst, sems.at[k])
        for k, (src, dst) in enumerate(((a, a_out), (b, b_out), (c, c_out)))
    ]
    for copy in copies:
        copy.start()
    for copy in copies:
        copy.wait()


def on_device(n, nseq, entering, fresh, qkv_first, qkv_second, rates_first, rates_second):
    rows, _, width = fresh.shape
    tokens = qkv_first.shape[1]
    m = min(8, rows // 16)
    period = max(m, 8)
    block = rows // m

    operands = [a.transpose(1, 0, 2) for a in (entering[0], fresh, qkv_first[0], qkv_second[0])]
    operands += [rates_first, rates_second]
    bf16, f32 = jnp.bfloat16, jnp.float32
    vmem = pl.BlockSpec(memory_space=pltpu.VMEM)
    hbm = pl.BlockSpec(memory_space=pltpu.HBM)
    rounds = 2 * m
    chunk = (3, block, width)
    dma = pltpu.SemaphoreType.DMA
    out_first, out_second, leaving = pl.pallas_call(
        functools.partial(kernel, n, nseq, m, period),
        out_shape=(
            jax.ShapeDtypeStruct((tokens, width), bf16),
            jax.ShapeDtypeStruct((tokens, width), bf16),
            jax.ShapeDtypeStruct((3, rows, width), bf16),
        ),
        in_specs=[hbm] * 6,
        out_specs=(vmem, vmem, vmem),
        scratch_shapes=[
            pltpu.VMEM((rounds, n) + chunk, bf16),
            pltpu.VMEM((rounds, n) + chunk, bf16),
            pltpu.VMEM((rounds, n) + chunk, bf16),
            pltpu.VMEM((4, n) + chunk, f32),
            pltpu.VMEM((2, 3, tokens, width), bf16),
            pltpu.VMEM((2, 3, width, tokens), bf16),
            pltpu.VMEM((tokens, width), f32),
            pltpu.VMEM((m,) + chunk, bf16),
            pltpu.VMEM((3, rows, width), bf16),
            pltpu.VMEM((2, 1, tokens), f32),
            dma((2,)),
            dma((2,)),
            dma((m,)),
            dma(()),
        ] + [dma((rounds, n))] * 7 + [dma((m,)), dma((m,))],
        compiler_params=pltpu.CompilerParams(
            collective_id=0, has_side_effects=True, vmem_limit_bytes=48 * 1024 * 1024),
    )(
        *(pltpu.with_memory_space_constraint(operand, pltpu.HBM) for operand in operands)
    )
    results = (out_first, out_second, leaving)
    out_first, out_second, leaving = pl.pallas_call(
        store_kernel,
        out_shape=tuple(jax.ShapeDtypeStruct(a.shape, a.dtype) for a in results),
        in_specs=[vmem] * 3,
        out_specs=(hbm,) * 3,
        scratch_shapes=[dma((3,))],
    )(*results)
    leaving = leaving.transpose(1, 0, 2)
    return (out_first[None], out_second[None], leaving[None])


def solution(mesh):
    placed = (
        P("seq", "tok", None, None),
        P("tok", None, None),
        P("seq", "tok", None, None),
        P("seq", "tok", None, None),
        P("seq", "tok"),
        P("seq", "tok"),
    )
    return jax.shard_map(
        functools.partial(on_device, mesh.shape["tok"], mesh.shape["seq"]),
        mesh=mesh,
        in_specs=placed,
        out_specs=(P("seq", "tok", None), P("seq", "tok", None), P("seq", "tok", None, None)),
        check_vma=False,
    )
```

```python
import functools
import jax
import jax.numpy as jnp
from jax import lax
from jax.experimental import pallas as pl
from jax.experimental.pallas import tpu as pltpu
from jax.sharding import PartitionSpec as P

MESH = pl.DeviceIdType.MESH
NN = (((1,), (0,)), ((), ()))


def dot(a, b, dims):
    return lax.dot_general(a, b, dims, preferred_element_type=jnp.float32)


def kernel(
    n, nseq, m, period,
    ent, fresh, x_first, x_second, rates_first, rates_second,
    out_first, out_second, leaving,
    wbuf, rl, rr, part, xbuf, flipped, acc, ubuf,
    fresh_buf, rates, rates_sem, x_sem, own_sem, fresh_sem, w_recv, w_send_r, w_send_l, rl_recv, rl_send, rr_recv, rr_send, n_send, n_recv,
):
    rounds = 2 * period
    s = lax.axis_index("seq")
    p = lax.axis_index("tok")
    when = pl.when
    has_left, has_right = p > 0, p < n - 1
    has_prev, has_next = s > 0, s < nseq - 1
    left, right = (s, jnp.maximum(p - 1, 0)), (s, jnp.minimum(p + 1, n - 1))
    prev, following = (jnp.maximum(s - 1, 0), p), (jnp.minimum(s + 1, nseq - 1), p)
    block, width = wbuf.shape[3:]
    units = n * block
    group = 2 if m % 2 == 0 else 1

    def rows(r):
        return pl.ds(pl.multiple_of(r * block, block), block)

    def load_x(t):
        src = x_first if t == 0 else x_second
        return pltpu.make_async_copy(src, xbuf.at[t], x_sem.at[t])

    def load_rates(t):
        return pltpu.make_async_copy((rates_first, rates_second)[t], rates.at[t], rates_sem.at[t])

    def load_own(r):
        return pltpu.make_async_copy(ent.at[:, r * block:(r + 1) * block], wbuf.at[r, p], own_sem.at[r])

    load_fresh = pltpu.make_async_copy(fresh, fresh_buf, fresh_sem)

    for r in range(m):
        load_own(r).start()

    barrier = pltpu.get_barrier_semaphore()
    for there, device in ((has_left, left), (has_right, right), (has_prev, prev), (has_next, following)):
        @when(there)
        def _():
            pl.semaphore_signal(barrier, inc=1, device_id=device, device_id_type=MESH)
    load_own(0).wait()
    peers = sum(jnp.where(there, 1, 0) for there in (has_left, has_right, has_prev, has_next))
    pl.semaphore_wait(barrier, peers)

    def valid(i):
        return jnp.logical_and(jnp.logical_and(i >= 0, i < rounds), lax.rem(i + 2 * period, period) < m)

    def index(i):
        return lax.div(i, period) * m + lax.rem(i, period)

    def w_right(g, j):
        return pltpu.make_async_remote_copy(
            wbuf.at[g, j], wbuf.at[g, j], w_send_r.at[g, j], w_recv.at[g, j], device_id=right, device_id_type=MESH)

    def w_left(g, j):
        return pltpu.make_async_remote_copy(
            wbuf.at[g, j], wbuf.at[g, j], w_send_l.at[g, j], w_recv.at[g, j], device_id=left, device_id_type=MESH)

    def sum_right(g, j):
        return pltpu.make_async_remote_copy(
            rl.at[g, j], rl.at[g, j], rl_send.at[g, j], rl_recv.at[g, j], device_id=right, device_id_type=MESH)

    def sum_left(g, j):
        return pltpu.make_async_remote_copy(
            rr.at[g, j], rr.at[g, j], rr_send.at[g, j], rr_recv.at[g, j], device_id=left, device_id_type=MESH)

    def hand_on(r):
        return pltpu.make_async_remote_copy(
            ubuf.at[r], wbuf.at[m + r, p], n_send.at[r], n_recv.at[r], device_id=following, device_id_type=MESH)

    def w_start(g):
        @when(g >= m)
        def _():
            @when(has_prev)
            def _():
                hand_on(g - m).wait_recv()

            @when(jnp.logical_not(has_prev))
            def _():
                wbuf[g, p] = fresh_buf[:, rows(g - m)]

        @when(has_right)
        def _():
            w_right(g, p).start()

        @when(has_left)
        def _():
            w_left(g, p).start()

    def w_hop(g, h):
        @when(p >= h)
        def _():
            w_right(g, p - h).wait_recv()

            @when(has_right)
            def _():
                w_right(g, p - h).start()

        @when(p + h < n)
        def _():
            w_left(g, p + h).wait_recv()

            @when(has_left)
            def _():
                w_left(g, p + h).start()

    def sum_hop(g, h):
        own = part.at[lax.rem(g, part.shape[0])]

        @when(p == h)
        def _():
            for j in range(n - 1, h, -1):
                value = own[j]
                if h > 0:
                    sum_right(g, j).wait_recv()
                    value = value + rl[g, j].astype(jnp.float32)
                rl[g, j] = value.astype(jnp.bfloat16)
                sum_right(g, j).start()

        @when(p == n - 1 - h)
        def _():
            for j in range(n - 1 - h):
                value = own[j]
                if h > 0:
                    sum_left(g, j).wait_recv()
                    value = value + rr[g, j].astype(jnp.float32)
                rr[g, j] = value.astype(jnp.bfloat16)
                sum_left(g, j).start()

    def update(g):
        for there, edge, buf, arrival in (
            (has_left, p == 0, rl, sum_right),
            (has_right, p == n - 1, rr, sum_left),
        ):
            @when(there)
            def _():
                arrival(g, p).wait_recv()

            @when(edge)
            def _():
                buf[g, p] = jnp.zeros(buf.shape[2:], buf.dtype)
        gradient = part[lax.rem(g, part.shape[0]), p] + rl[g, p].astype(jnp.float32) + rr[g, p].astype(jnp.float32)
        old = wbuf[g, p].astype(jnp.float32)
        stepped = old - gradient
        old_norm = jnp.sqrt(jnp.sum(old * old, axis=-1, keepdims=True))
        new_norm = jnp.sqrt(jnp.sum(stepped * stepped, axis=-1, keepdims=True) + 1e-06)
        new = (stepped * (old_norm / new_norm)).astype(jnp.bfloat16)

        @when(g < m)
        def _():
            ubuf[g] = new

            @when(has_next)
            def _():
                hand_on(g).start()

        @when(g >= m)
        def _():
            leaving[:, rows(g - m)] = new

    def prepare(t):
        load_x(t).wait()
        load_rates(t).wait()
        column = jnp.broadcast_to(rates[t], (8, rates.shape[2])).T[:, 0:1]
        xbuf[t, 2] = (-column * xbuf[t, 2].astype(jnp.float32)).astype(jnp.bfloat16)
        for c in range(3):
            flipped[t, c] = xbuf[t, c].T

    def key_part(g):
        t = lax.div(g, m)
        keys, scaled = xbuf[t, 1], xbuf[t, 2]
        w_gu = wbuf[g, :, 0:2].reshape(2 * units, width)
        w_d = wbuf[g, :, 2].reshape(units, width)
        pre = dot(w_gu, flipped[t, 1], NN).reshape(n, 2, block, -1)
        gate, up = pre[:, 0], pre[:, 1]
        d_hidden = dot(w_d, flipped[t, 2], NN).reshape(gate.shape)
        sig = 1.0 / (1.0 + jnp.exp(-gate))
        act = gate * sig
        hidden = (act * up).astype(jnp.bfloat16).reshape(units, -1)
        d_gate = (d_hidden * up * (sig * (1.0 + gate * (1.0 - sig)))).astype(jnp.bfloat16)
        d_up = (d_hidden * act).astype(jnp.bfloat16)
        d_gu = jnp.stack([d_gate, d_up], axis=1).reshape(2 * units, -1)
        place = lax.rem(g, part.shape[0])
        part[place, :, 0:2] = dot(d_gu, keys, NN).reshape(n, 2, block, width)
        part[place, :, 2] = dot(hidden, scaled, NN).reshape(n, block, width)

    def query_part(g):
        t = lax.div(g, m)
        r = lax.rem(g, m)

        def of(c):
            return [wbuf[g - k, :, c].reshape(units, width) for k in range(group)]

        count = group * units
        pre = dot(jnp.concatenate(of(0) + of(1), axis=0), flipped[t, 0], NN)
        gate, up = pre[:count], pre[count:]
        hidden = (gate / (1.0 + jnp.exp(-gate)) * up).astype(jnp.bfloat16)
        out = dot(hidden.T, jnp.concatenate(of(2), axis=0), NN)

        @when(r == group - 1)
        def _():
            acc[...] = out

        @when(r > group - 1)
        def _():
            acc[...] += out

        @when(r == m - 1)
        def _():
            @when(t == 0)
            def _():
                out_first[...] = acc[...].astype(jnp.bfloat16)

            @when(t == 1)
            def _():
                out_second[...] = acc[...].astype(jnp.bfloat16)

    def drain(g):
        for j in range(n):
            @when(jnp.logical_and(j <= p, has_right))
            def _():
                w_right(g, j).wait_send()

            @when(jnp.logical_and(j >= p, has_left))
            def _():
                w_left(g, j).wait_send()

            @when(j > p)
            def _():
                sum_right(g, j).wait_send()

            @when(j < p)
            def _():
                sum_left(g, j).wait_send()

        @when(jnp.logical_and(g < m, has_next))
        def _():
            hand_on(g).wait_send()

    def thirds(hops):
        size = -(-len(hops) // 3)
        return hops[:size], hops[size:2 * size], hops[2 * size:]

    w_hops = thirds(range(1, n))
    s_hops = thirds(range(1, n - 1))

    w_start(0)
    for t in range(2):
        load_x(t).start()
        load_rates(t).start()
    load_fresh.start()
    for r in range(1, m):
        load_own(r).wait()

    def slot(step, carry):
        i = step - 2

        @when(valid(i + 3))
        def _():
            w_start(index(i + 3))

        for ahead, hops in zip((2, 1, 0), w_hops):
            @when(valid(i + ahead))
            def _():
                for h in hops:
                    w_hop(index(i + ahead), h)

        for t in range(2):
            @when(i == t - 2)
            def _():
                prepare(t)
                if t == 1:
                    load_fresh.wait()

        @when(valid(i - 5))
        def _():
            drain(index(i - 5))

        for behind, hops in zip((2, 3, 4), s_hops):
            @when(valid(i - behind))
            def _():
                for h in hops:
                    sum_hop(index(i - behind), h)

        @when(valid(i - 4))
        def _():
            update(index(i - 4))

        @when(valid(i))
        def _():
            key_part(index(i))
            sum_hop(index(i), 0)

        @when(jnp.logical_and(valid(i - 1), lax.rem(lax.rem(i - 1 + period, period), group) == group - 1))
        def _():
            query_part(index(i - 1))

        return carry

    lax.fori_loop(0, rounds + 6, slot, 0)

    if (rounds - 1) % period < m:
        drain(2 * m - 1)


def on_device(n, nseq, entering, fresh, qkv_first, qkv_second, rates_first, rates_second):
    rows, _, width = fresh.shape
    tokens = qkv_first.shape[1]
    m = min(8, rows // 16)
    period = max(m, 8)
    block = rows // m

    operands = [a.transpose(1, 0, 2) for a in (entering[0], fresh, qkv_first[0], qkv_second[0])]
    operands += [rates_first, rates_second]
    bf16, f32 = jnp.bfloat16, jnp.float32
    vmem = pl.BlockSpec(memory_space=pltpu.VMEM)
    hbm = pl.BlockSpec(memory_space=pltpu.HBM)
    rounds = 2 * m
    chunk = (3, block, width)
    dma = pltpu.SemaphoreType.DMA
    out_first, out_second, leaving = pl.pallas_call(
        functools.partial(kernel, n, nseq, m, period),
        out_shape=(
            jax.ShapeDtypeStruct((tokens, width), bf16),
            jax.ShapeDtypeStruct((tokens, width), bf16),
            jax.ShapeDtypeStruct((3, rows, width), bf16),
        ),
        in_specs=[hbm] * 6,
        out_specs=(vmem, vmem, vmem),
        scratch_shapes=[
            pltpu.VMEM((rounds, n) + chunk, bf16),
            pltpu.VMEM((rounds, n) + chunk, bf16),
            pltpu.VMEM((rounds, n) + chunk, bf16),
            pltpu.VMEM((4, n) + chunk, f32),
            pltpu.VMEM((2, 3, tokens, width), bf16),
            pltpu.VMEM((2, 3, width, tokens), bf16),
            pltpu.VMEM((tokens, width), f32),
            pltpu.VMEM((m,) + chunk, bf16),
            pltpu.VMEM((3, rows, width), bf16),
            pltpu.VMEM((2, 1, tokens), f32),
            dma((2,)),
            dma((2,)),
            dma((m,)),
            dma(()),
        ] + [dma((rounds, n))] * 7 + [dma((m,)), dma((m,))],
        compiler_params=pltpu.CompilerParams(
            collective_id=0, has_side_effects=True, vmem_limit_bytes=48 * 1024 * 1024),
    )(
        *(pltpu.with_memory_space_constraint(operand, pltpu.HBM) for operand in operands)
    )
    leaving = leaving.transpose(1, 0, 2)
    return (out_first[None], out_second[None], leaving[None])


def solution(mesh):
    placed = (
        P("seq", "tok", None, None),
        P("tok", None, None),
        P("seq", "tok", None, None),
        P("seq", "tok", None, None),
        P("seq", "tok"),
        P("seq", "tok"),
    )
    return jax.shard_map(
        functools.partial(on_device, mesh.shape["tok"], mesh.shape["seq"]),
        mesh=mesh,
        in_specs=placed,
        out_specs=(P("seq", "tok", None), P("seq", "tok", None), P("seq", "tok", None, None)),
        check_vma=False,
    )
```

```python
import functools
import jax
import jax.numpy as jnp
from jax import lax
from jax.experimental import pallas as pl
from jax.experimental.pallas import tpu as pltpu
from jax.sharding import PartitionSpec as P

MESH = pl.DeviceIdType.MESH
NN = (((1,), (0,)), ((), ()))


def dot(a, b, dims):
    return lax.dot_general(a, b, dims, preferred_element_type=jnp.float32)


def kernel(
    n, nseq, m, period,
    ent, fresh, x_first, x_second, rates_first, rates_second,
    out_first, out_second, leaving,
    wbuf, rl, rr, part, xbuf, flipped, acc, ubuf,
    fresh_buf, rates, rates_sem, x_sem, own_sem, fresh_sem, w_recv, w_send_r, w_send_l, rl_recv, rl_send, rr_recv, rr_send, n_send, n_recv,
):
    rounds = 2 * period
    s = lax.axis_index("seq")
    p = lax.axis_index("tok")
    when = pl.when
    has_left, has_right = p > 0, p < n - 1
    has_prev, has_next = s > 0, s < nseq - 1
    left, right = (s, jnp.maximum(p - 1, 0)), (s, jnp.minimum(p + 1, n - 1))
    prev, following = (jnp.maximum(s - 1, 0), p), (jnp.minimum(s + 1, nseq - 1), p)
    block, width = wbuf.shape[3:]
    units = n * block
    group = 2 if m % 2 == 0 else 1

    def rows(r):
        return pl.ds(pl.multiple_of(r * block, block), block)

    def load_x(t):
        src = x_first if t == 0 else x_second
        return pltpu.make_async_copy(src, xbuf.at[t], x_sem.at[t])

    def load_rates(t):
        return pltpu.make_async_copy((rates_first, rates_second)[t], rates.at[t], rates_sem.at[t])

    def load_own(r):
        return pltpu.make_async_copy(ent.at[:, r * block:(r + 1) * block], wbuf.at[r, p], own_sem.at[r])

    load_fresh = pltpu.make_async_copy(fresh, fresh_buf, fresh_sem)

    for r in range(m):
        load_own(r).start()

    barrier = pltpu.get_barrier_semaphore()
    for there, device in ((has_left, left), (has_right, right), (has_prev, prev), (has_next, following)):
        @when(there)
        def _():
            pl.semaphore_signal(barrier, inc=1, device_id=device, device_id_type=MESH)
    load_own(0).wait()
    peers = sum(jnp.where(there, 1, 0) for there in (has_left, has_right, has_prev, has_next))
    pl.semaphore_wait(barrier, peers)

    def valid(i):
        return jnp.logical_and(jnp.logical_and(i >= 0, i < rounds), lax.rem(i + 2 * period, period) < m)

    def index(i):
        return lax.div(i, period) * m + lax.rem(i, period)

    def w_right(g, j):
        return pltpu.make_async_remote_copy(
            wbuf.at[g, j], wbuf.at[g, j], w_send_r.at[g, j], w_recv.at[g, j], device_id=right, device_id_type=MESH)

    def w_left(g, j):
        return pltpu.make_async_remote_copy(
            wbuf.at[g, j], wbuf.at[g, j], w_send_l.at[g, j], w_recv.at[g, j], device_id=left, device_id_type=MESH)

    def sum_right(g, j):
        return pltpu.make_async_remote_copy(
            rl.at[g, j], rl.at[g, j], rl_send.at[g, j], rl_recv.at[g, j], device_id=right, device_id_type=MESH)

    def sum_left(g, j):
        return pltpu.make_async_remote_copy(
            rr.at[g, j], rr.at[g, j], rr_send.at[g, j], rr_recv.at[g, j], device_id=left, device_id_type=MESH)

    def hand_on(r):
        return pltpu.make_async_remote_copy(
            ubuf.at[r], wbuf.at[m + r, p], n_send.at[r], n_recv.at[r], device_id=following, device_id_type=MESH)

    def w_start(g):
        @when(g >= m)
        def _():
            @when(has_prev)
            def _():
                hand_on(g - m).wait_recv()

            @when(jnp.logical_not(has_prev))
            def _():
                wbuf[g, p] = fresh_buf[:, rows(g - m)]

        @when(has_right)
        def _():
            w_right(g, p).start()

        @when(has_left)
        def _():
            w_left(g, p).start()

    def w_hop(g, h):
        @when(p >= h)
        def _():
            w_right(g, p - h).wait_recv()

            @when(has_right)
            def _():
                w_right(g, p - h).start()

        @when(p + h < n)
        def _():
            w_left(g, p + h).wait_recv()

            @when(has_left)
            def _():
                w_left(g, p + h).start()

    def sum_hop(g, h):
        own = part.at[lax.rem(g, part.shape[0])]

        @when(p == h)
        def _():
            for j in range(n - 1, h, -1):
                value = own[j]
                if h > 0:
                    sum_right(g, j).wait_recv()
                    value = value + rl[g, j].astype(jnp.float32)
                rl[g, j] = value.astype(jnp.bfloat16)
                sum_right(g, j).start()

        @when(p == n - 1 - h)
        def _():
            for j in range(n - 1 - h):
                value = own[j]
                if h > 0:
                    sum_left(g, j).wait_recv()
                    value = value + rr[g, j].astype(jnp.float32)
                rr[g, j] = value.astype(jnp.bfloat16)
                sum_left(g, j).start()

    def update(g):
        for there, edge, buf, arrival in (
            (has_left, p == 0, rl, sum_right),
            (has_right, p == n - 1, rr, sum_left),
        ):
            @when(there)
            def _():
                arrival(g, p).wait_recv()

            @when(edge)
            def _():
                buf[g, p] = jnp.zeros(buf.shape[2:], buf.dtype)
        gradient = part[lax.rem(g, part.shape[0]), p] + rl[g, p].astype(jnp.float32) + rr[g, p].astype(jnp.float32)
        old = wbuf[g, p].astype(jnp.float32)
        stepped = old - gradient
        old_norm = jnp.sqrt(jnp.sum(old * old, axis=-1, keepdims=True))
        new_norm = jnp.sqrt(jnp.sum(stepped * stepped, axis=-1, keepdims=True) + 1e-06)
        new = (stepped * (old_norm / new_norm)).astype(jnp.bfloat16)

        @when(g < m)
        def _():
            ubuf[g] = new

            @when(has_next)
            def _():
                hand_on(g).start()

        @when(g >= m)
        def _():
            leaving[:, rows(g - m)] = new

    def prepare(t):
        load_x(t).wait()
        load_rates(t).wait()
        column = jnp.broadcast_to(rates[t], (8, rates.shape[2])).T[:, 0:1]
        xbuf[t, 2] = (-column * xbuf[t, 2].astype(jnp.float32)).astype(jnp.bfloat16)
        for c in (1, 2):
            flipped[t, c] = xbuf[t, c].T

    def key_part(g):
        t = lax.div(g, m)
        keys, scaled = xbuf[t, 1], xbuf[t, 2]
        w_gu = wbuf[g, :, 0:2].reshape(2 * units, width)
        w_d = wbuf[g, :, 2].reshape(units, width)
        pre = dot(w_gu, flipped[t, 1], NN).reshape(n, 2, block, -1)
        gate, up = pre[:, 0], pre[:, 1]
        d_hidden = dot(w_d, flipped[t, 2], NN).reshape(gate.shape)
        sig = 1.0 / (1.0 + jnp.exp(-gate))
        act = gate * sig
        hidden = (act * up).astype(jnp.bfloat16).reshape(units, -1)
        d_gate = (d_hidden * up * (sig * (1.0 + gate * (1.0 - sig)))).astype(jnp.bfloat16)
        d_up = (d_hidden * act).astype(jnp.bfloat16)
        d_gu = jnp.stack([d_gate, d_up], axis=1).reshape(2 * units, -1)
        place = lax.rem(g, part.shape[0])
        part[place, :, 0:2] = dot(d_gu, keys, NN).reshape(n, 2, block, width)
        part[place, :, 2] = dot(hidden, scaled, NN).reshape(n, block, width)

    def query_part(g):
        t = lax.div(g, m)
        r = lax.rem(g, m)

        def of(c):
            return [wbuf[g - k, :, c].reshape(units, width) for k in range(group)]

        count = group * units
        pre = dot(jnp.concatenate(of(0) + of(1), axis=0), flipped[t, 0], NN)
        gate, up = pre[:count], pre[count:]
        hidden = (gate / (1.0 + jnp.exp(-gate)) * up).astype(jnp.bfloat16)
        out = dot(hidden.T, jnp.concatenate(of(2), axis=0), NN)

        @when(r == group - 1)
        def _():
            acc[...] = out

        @when(r > group - 1)
        def _():
            acc[...] += out

        @when(r == m - 1)
        def _():
            @when(t == 0)
            def _():
                out_first[...] = acc[...].astype(jnp.bfloat16)

            @when(t == 1)
            def _():
                out_second[...] = acc[...].astype(jnp.bfloat16)

    def drain(g):
        for j in range(n):
            @when(jnp.logical_and(j <= p, has_right))
            def _():
                w_right(g, j).wait_send()

            @when(jnp.logical_and(j >= p, has_left))
            def _():
                w_left(g, j).wait_send()

            @when(j > p)
            def _():
                sum_right(g, j).wait_send()

            @when(j < p)
            def _():
                sum_left(g, j).wait_send()

        @when(jnp.logical_and(g < m, has_next))
        def _():
            hand_on(g).wait_send()

    def thirds(hops):
        size = -(-len(hops) // 3)
        return hops[:size], hops[size:2 * size], hops[2 * size:]

    w_hops = thirds(range(1, n))
    s_hops = thirds(range(1, n - 1))

    w_start(0)
    for t in range(2):
        load_x(t).start()
        load_rates(t).start()
    load_fresh.start()
    for r in range(1, m):
        load_own(r).wait()

    def slot(step, carry):
        i = step - 2

        @when(valid(i + 3))
        def _():
            w_start(index(i + 3))

        for ahead, hops in zip((2, 1, 0), w_hops):
            @when(valid(i + ahead))
            def _():
                for h in hops:
                    w_hop(index(i + ahead), h)

        for t in range(2):
            begin = (-2, period - 4)[t]

            @when(i == begin)
            def _():
                prepare(t)

            @when(i == begin + 1)
            def _():
                flipped[t, 0] = xbuf[t, 0].T
                if t == 0:
                    load_fresh.wait()

        @when(valid(i - 5))
        def _():
            drain(index(i - 5))

        for behind, hops in zip((2, 3, 4), s_hops):
            @when(valid(i - behind))
            def _():
                for h in hops:
                    sum_hop(index(i - behind), h)

        @when(valid(i - 4))
        def _():
            update(index(i - 4))

        @when(valid(i))
        def _():
            key_part(index(i))
            sum_hop(index(i), 0)

        @when(jnp.logical_and(valid(i - 1), lax.rem(lax.rem(i - 1 + period, period), group) == group - 1))
        def _():
            query_part(index(i - 1))

        return carry

    lax.fori_loop(0, rounds + 6, slot, 0)

    if (rounds - 1) % period < m:
        drain(2 * m - 1)


def on_device(n, nseq, entering, fresh, qkv_first, qkv_second, rates_first, rates_second):
    rows, _, width = fresh.shape
    tokens = qkv_first.shape[1]
    m = min(8, rows // 16)
    period = max(m, 8)
    block = rows // m

    operands = [a.transpose(1, 0, 2) for a in (entering[0], fresh, qkv_first[0], qkv_second[0])]
    operands += [rates_first, rates_second]
    bf16, f32 = jnp.bfloat16, jnp.float32
    vmem = pl.BlockSpec(memory_space=pltpu.VMEM)
    hbm = pl.BlockSpec(memory_space=pltpu.HBM)
    rounds = 2 * m
    chunk = (3, block, width)
    dma = pltpu.SemaphoreType.DMA
    out_first, out_second, leaving = pl.pallas_call(
        functools.partial(kernel, n, nseq, m, period),
        out_shape=(
            jax.ShapeDtypeStruct((tokens, width), bf16),
            jax.ShapeDtypeStruct((tokens, width), bf16),
            jax.ShapeDtypeStruct((3, rows, width), bf16),
        ),
        in_specs=[hbm] * 6,
        out_specs=(vmem, vmem, vmem),
        scratch_shapes=[
            pltpu.VMEM((rounds, n) + chunk, bf16),
            pltpu.VMEM((rounds, n) + chunk, bf16),
            pltpu.VMEM((rounds, n) + chunk, bf16),
            pltpu.VMEM((4, n) + chunk, f32),
            pltpu.VMEM((2, 3, tokens, width), bf16),
            pltpu.VMEM((2, 3, width, tokens), bf16),
            pltpu.VMEM((tokens, width), f32),
            pltpu.VMEM((m,) + chunk, bf16),
            pltpu.VMEM((3, rows, width), bf16),
            pltpu.VMEM((2, 1, tokens), f32),
            dma((2,)),
            dma((2,)),
            dma((m,)),
            dma(()),
        ] + [dma((rounds, n))] * 7 + [dma((m,)), dma((m,))],
        compiler_params=pltpu.CompilerParams(
            collective_id=0, has_side_effects=True, vmem_limit_bytes=48 * 1024 * 1024),
    )(
        *(pltpu.with_memory_space_constraint(operand, pltpu.HBM) for operand in operands)
    )
    leaving = leaving.transpose(1, 0, 2)
    return (out_first[None], out_second[None], leaving[None])


def solution(mesh):
    placed = (
        P("seq", "tok", None, None),
        P("tok", None, None),
        P("seq", "tok", None, None),
        P("seq", "tok", None, None),
        P("seq", "tok"),
        P("seq", "tok"),
    )
    return jax.shard_map(
        functools.partial(on_device, mesh.shape["tok"], mesh.shape["seq"]),
        mesh=mesh,
        in_specs=placed,
        out_specs=(P("seq", "tok", None), P("seq", "tok", None), P("seq", "tok", None, None)),
        check_vma=False,
    )
```
